512 devices in a mesh: grp: 64 (over y, z_hi, core), tp: 8 (over x, z_lo).
Axes of the slice: x: 4, y: 8, z: 8 (z_hi: 4, z_lo: 2; z = z_hi * 2 + z_lo), core: 2. Of those that a mesh axis runs over, the one named last changes fastest.
Arguments:
- learn_rows: bfloat16 [98304, 5120], P('grp', 'tp'), may hold values from -6 to 6
- cot_values: bfloat16 [98304, 1024], P('grp', 'tp'), may hold values from -60 to 60
- rewards: float32 [98304], P('grp'), may hold values from 0 to 4
- group_ids: int32 [98304], P('grp'), may hold values from 0 to 255
- master: float32 [1024, 5120], P('grp', 'tp'), may hold values from -0.078125 to 0.078125
- moment_one: float32 [1024, 5120], P('grp', 'tp'), may hold values from -2 to 2
- moment_two: float32 [1024, 5120], P('grp', 'tp'), may hold values from 0.041666668 to 4.1666665
- decode_rows: bfloat16 [512, 5120], P('grp'), may hold values from -6 to 6
- queries: bfloat16 [512, 8192], P('grp', 'tp'), may hold values from -100 to 100
- fresh_keys: bfloat16 [512, 1024], P('grp', 'tp'), may hold values from -4.04 to 4.04
- stored_keys: bfloat16 [512, 256, 1024], P('grp', None, 'tp'), may hold values from -4 to 4
- stored_values: bfloat16 [512, 256, 1024], P('grp', None, 'tp'), may hold values from -6 to 6
- cache_lengths: int32 [512], P('grp'), may hold values from 1 to 256, as said below
Outputs:
- new_master: float32 [1024, 5120], P('grp', 'tp')
- new_moment_one: float32 [1024, 5120], P('grp', 'tp')
- new_moment_two: float32 [1024, 5120], P('grp', 'tp')
- attended: bfloat16 [512, 8192], P('grp', 'tp')
The draws below stay inside these ranges and needn't reach their ends.
Inputs may be any that keep to these rules, and one draw needn't show every extreme that they name: `cache_lengths`: row 0 of every draw holds 256.
All inputs are finite; a program needn't handle non-finite values.
Results may differ from the reference program's by a relative error of at most 0.013.
Values may be sent and summed in bfloat16 or wider, within the bound.
A program may use at most 64 MiB of HBM per device.

```python
import math
import jax
import jax.numpy as jnp
from jax import lax

D = 5120
QUERY_HEADS = 64
KEY_VALUE_HEADS = 8
HEAD_SIZE = 128
LROWS_DEV = 1536
CACHED_SLOTS = 256
KVW = 1024
LROWS = 98304
NGROUP = 256
DECODE_TOTAL = 512


def cache_base(key):
    return jnp.clip(jax.random.normal(jax.random.fold_in(key, 11), (DECODE_TOTAL, CACHED_SLOTS, KEY_VALUE_HEADS * HEAD_SIZE), jnp.float32), -4.0, 4.0)


def draw_stored_keys(key, part):
    shared_heads = cache_base(key)
    return shared_heads.astype(jnp.bfloat16)


def draw_queries(key, part):
    key = jax.random.fold_in(key, 5)
    final_result = jax.random.normal(key, (DECODE_TOTAL, QUERY_HEADS * HEAD_SIZE), jnp.float32)
    return final_result.astype(jnp.bfloat16)


def draw_fresh_keys(key, part):
    key = jax.random.fold_in(key, 7)
    final_result = jnp.clip(jax.random.normal(key, (DECODE_TOTAL, KEY_VALUE_HEADS * HEAD_SIZE), jnp.float32), -4.0, 4.0)
    return final_result.astype(jnp.bfloat16)


def draw_cache_lengths(key, part):
    key = jax.random.fold_in(key, 9)
    drawn = jax.random.randint(key, (DECODE_TOTAL,), 1, CACHED_SLOTS + 1, jnp.int32)
    return drawn.at[0].set(CACHED_SLOTS)


def with_ends(result, key, smallest, high):
    index_at = [jax.random.randint(jax.random.fold_in(key, axis), (), 0, length) for axis, length in enumerate(result.shape)]
    main_axis = result.shape.index(max(result.shape))
    beside = index_at[:main_axis] + [(index_at[main_axis] + 1) % result.shape[main_axis]] + index_at[main_axis + 1:]
    return result.at[tuple(index_at)].set(smallest).at[tuple(beside)].set(high)


def block_levels(own_key, extent, split, least, high):
    level, own = 1.0, jax.random.fold_in(own_key, 6)
    for axis_at, blocks in split:
        heights = jnp.exp(jax.random.uniform(jax.random.fold_in(own, axis_at), (blocks,), jnp.float32, least / len(split), high / len(split)))
        level = level * jnp.repeat(heights, extent[axis_at] // blocks).reshape([-1 if axis == axis_at else 1 for axis in range(len(extent))])
    return level


def bell_draw(own_key, extent, width, limit, cuts=(), kind=jnp.bfloat16):
    factor_of = block_levels(own_key, extent, cuts, -0.22, 0.18) if cuts else 1.0
    array = jax.random.normal(own_key, extent, jnp.float32) * width * factor_of
    return jnp.minimum(jnp.maximum(array, -limit), limit).astype(kind)


def setup_inputs(seed: int = 0) -> dict:
    keys = jax.random.split(jax.random.key(seed), 14)
    return {
        "learn_rows": bell_draw(keys[0], (LROWS, D), 1.0, 6.0, ((0, 64), (1, 8))),
        "cot_values": bell_draw(keys[1], (LROWS, KVW), 10.0, 60.0, ((0, 64), (1, 8))),
        "rewards": jnp.clip(4.0 * jax.random.uniform(keys[2], (LROWS,), jnp.float32) ** block_levels(keys[2], (LROWS,), ((0, 64),), -0.2, 0.2), 0.0, 4.0),
        "group_ids": with_ends(jax.random.randint(keys[3], (LROWS,), 0, NGROUP), jax.random.fold_in(keys[3], 1), 0, NGROUP - 1).astype(jnp.int32),
        "master": bell_draw(keys[4], (KVW, D), D ** -0.5, 0.078125, ((0, 64), (1, 8)), jnp.float32),
        "moment_one": bell_draw(keys[5], (KVW, D), 0.3, 2.0, ((0, 64), (1, 8)), jnp.float32),
        "moment_two": jnp.clip(jnp.exp(math.log(4.1666665) - 4.6051701 * jax.random.uniform(keys[6], (KVW, D), jnp.float32) ** block_levels(keys[6], (KVW, D), ((0, 64), (1, 8)), -0.2, 0.2)), 0.041666668, 4.1666665),
        "decode_rows": bell_draw(keys[7], (DECODE_TOTAL, D), 1.0, 6.0, ((0, 64),)),
        "queries": draw_queries(jax.random.fold_in(keys[13], 71), 0),
        "fresh_keys": draw_fresh_keys(jax.random.fold_in(keys[13], 71), 0),
        "stored_keys": draw_stored_keys(jax.random.fold_in(keys[13], 71), 0),
        "stored_values": bell_draw(keys[11], (DECODE_TOTAL, CACHED_SLOTS, KVW), 1.0, 6.0, ((0, 64), (2, 8))),
        "cache_lengths": draw_cache_lengths(jax.random.fold_in(keys[13], 71), 0),
    }


beta_one = 0.9
beta_two = 0.95
learning_rate = 0.001
weight_decay = 0.1
adam_epsilon = 1e-08
step_count = 2.0

def reference(learn_rows, cot_values, rewards, group_ids, master, moment_one, moment_two, decode_rows, queries, fresh_keys, stored_keys, stored_values, cache_lengths):
    highest = lax.Precision.HIGHEST
    onehot = (group_ids[:, None] == jnp.arange(NGROUP, dtype=jnp.int32)[None, :]).astype(jnp.float32)
    totals = jnp.dot(rewards, onehot, precision=highest)
    members = lax.optimization_barrier(jnp.sum(onehot, axis=0))
    advantage = rewards - jnp.dot(onehot, totals, precision=highest) / jnp.dot(onehot, members, precision=highest)
    weighted = (advantage[:, None] * cot_values.astype(jnp.float32) / LROWS_DEV).astype(jnp.bfloat16)
    gradient = lax.dot_general(weighted, learn_rows, (((0,), (0,)), ((), ())), preferred_element_type=jnp.float32)
    first = beta_one * moment_one + (1.0 - beta_one) * gradient
    second = beta_two * moment_two + (1.0 - beta_two) * gradient * gradient
    first_hat = first / (1.0 - beta_one ** step_count)
    second_hat = second / (1.0 - beta_two ** step_count)
    updated = master - learning_rate * (first_hat / (jnp.sqrt(second_hat) + adam_epsilon) + weight_decay * master)
    refreshed = updated.astype(jnp.bfloat16)
    fresh_values = lax.dot_general(decode_rows, refreshed, (((1,), (1,)), ((), ())), preferred_element_type=jnp.float32).astype(jnp.bfloat16)
    row_sum_total = queries.shape[0]
    heads_per_group = QUERY_HEADS // KEY_VALUE_HEADS
    scale_factor = 1.0 / math.sqrt(HEAD_SIZE)
    query_tiles = queries.astype(jnp.float32).reshape(row_sum_total, KEY_VALUE_HEADS, heads_per_group, HEAD_SIZE)
    key_tiles = stored_keys.astype(jnp.float32).reshape(row_sum_total, CACHED_SLOTS, KEY_VALUE_HEADS, HEAD_SIZE)
    value_tiles = stored_values.astype(jnp.float32).reshape(row_sum_total, CACHED_SLOTS, KEY_VALUE_HEADS, HEAD_SIZE)
    scores = jnp.einsum('rhgd,rlhd->rhgl', query_tiles, key_tiles) * scale_factor
    visible = (jnp.arange(CACHED_SLOTS, dtype=jnp.int32)[None, :] < cache_lengths[:, None])[:, None, None, :]
    scores = jnp.where(visible, scores, -jnp.inf)
    self_score = jnp.einsum('qvpb,qvb->qvp', query_tiles, fresh_keys.astype(jnp.float32).reshape(row_sum_total, KEY_VALUE_HEADS, HEAD_SIZE)) * scale_factor
    highest_score = jnp.maximum(lax.optimization_barrier(jnp.max(scores, axis=-1)), self_score)
    cache_exp = jnp.exp(scores - highest_score[..., None])
    own_exp = jnp.exp(self_score - highest_score)
    denominator = lax.optimization_barrier(jnp.sum(cache_exp, axis=-1)) + own_exp
    cache_weights = (cache_exp / denominator[..., None]).astype(jnp.bfloat16)
    self_weight = (own_exp / denominator).astype(jnp.bfloat16)
    output_rows = jnp.einsum('rhgl,rlhd->rhgd', cache_weights.astype(jnp.float32), value_tiles)
    output_rows = output_rows + self_weight.astype(jnp.float32)[..., None] * fresh_values.astype(jnp.float32).reshape(row_sum_total, KEY_VALUE_HEADS, 1, HEAD_SIZE)
    attended = output_rows.reshape(row_sum_total, QUERY_HEADS * HEAD_SIZE).astype(jnp.bfloat16)
    return (updated, first, second, attended)
```

```python
import math

import jax
import jax.numpy as jnp
from jax import lax
from jax.experimental import pallas as pl
from jax.experimental.pallas import tpu as pltpu
from jax.sharding import PartitionSpec as P

HEAD_SIZE = 128
QUERIES = 8
ROWS = 1536
WIDTH = 640
GROUPS = 256
SLOTS = 256
DECODE = 8
Y, ZH, CORE, X, ZL = 8, 4, 2, 4, 2
TP = X * ZL
BLOCKS = 8
BLOCK = 16
HALF = 64
WIDE = 3

beta_one = 0.9
beta_two = 0.95
learning_rate = 0.001
weight_decay = 0.1
adam_epsilon = 1e-08
step_count = 2.0

MESH = pl.DeviceIdType.MESH
bf16, f32 = jnp.bfloat16, jnp.float32


def split_three(value):
    high = value.astype(bf16)
    rest = value - high.astype(f32)
    middle = rest.astype(bf16)
    low = (rest - middle.astype(f32)).astype(bf16)
    return high, middle, low


def optimizer_step(gradient, master, moment_one, moment_two):
    first = beta_one * moment_one + (1.0 - beta_one) * gradient
    second = beta_two * moment_two + (1.0 - beta_two) * gradient * gradient
    first_hat = first / (1.0 - beta_one**step_count)
    second_hat = second / (1.0 - beta_two**step_count)
    updated = master - learning_rate * (
        first_hat / (jnp.sqrt(second_hat) + adam_epsilon) + weight_decay * master
    )
    return updated, first, second


def dot(a, b, dims):
    return lax.dot_general(a, b, (dims, ((), ())), preferred_element_type=f32)


def kernel(
    cot_hbm,
    learn_hbm,
    rewards_hbm,
    ids_hbm,
    master_hbm,
    one_hbm,
    two_hbm,
    decode_hbm,
    queries_hbm,
    fresh_hbm,
    keys_hbm,
    values_hbm,
    lengths_ref,
    gradient_hbm,
    attended_hbm,
    cot,
    learn,
    rewards,
    ids,
    adam_in,
    decode_own,
    queries,
    fresh,
    keys,
    values,
    attended,
    gathered,
    member,
    totals_out,
    totals_core,
    totals_z,
    totals_y,
    decode_all,
    weights,
    cache_part,
    own_part,
    kept,
    core_out,
    core_in,
    z_out,
    z_in,
    y_out,
    y_in,
    wide_out,
    wide_in,
    own_sum,
    fresh_rows,
    part_out,
    part_in,
    load_sem,
    store_sem,
    ag_send,
    ag_recv,
    core_send,
    core_recv,
    z_send,
    z_recv,
    y_send,
    y_recv,
    row_send,
    row_recv,
    part_send,
    part_recv,
    tot_send,
    tot_recv,
    dec_send,
    dec_recv,
):
    g, t = lax.axis_index("grp"), lax.axis_index("tp")
    y, zh, core = g // (ZH * CORE), lax.rem(g // CORE, ZH), lax.rem(g, CORE)
    x, zl = t // ZL, lax.rem(t, ZL)

    def grp_of(y_at, zh_at, core_at):
        return (y_at * ZH + zh_at) * CORE + core_at

    def tp_of(x_off, flip):
        return lax.rem(x + x_off + X, X) * ZL + lax.rem(zl + flip, ZL)

    right, left, across = tp_of(1, 0), tp_of(-1, 0), tp_of(0, 1)

    def remote(src, dst, send, recv, device):
        return pltpu.make_async_remote_copy(
            src_ref=src,
            dst_ref=dst,
            send_sem=send,
            recv_sem=recv,
            device_id=device,
            device_id_type=MESH,
        )

    loads = [
        (cot_hbm, cot),
        (ids_hbm, ids),
        (rewards_hbm, rewards),
        (queries_hbm, queries),
        (fresh_hbm, fresh),
        (keys_hbm, keys),
        (decode_hbm.at[:, pl.ds(pl.multiple_of(t * WIDTH, 128), WIDTH)], decode_own),
        (learn_hbm, learn),
        (values_hbm, values),
        (master_hbm, adam_in.at[0]),
        (one_hbm, adam_in.at[1]),
        (two_hbm, adam_in.at[2]),
    ]
    loads = [pltpu.make_async_copy(src, dst, load_sem.at[i]) for i, (src, dst) in enumerate(loads)]
    for load in loads:
        load.start()
    (l_cot, l_ids, l_rewards, l_queries, l_fresh, l_keys, l_decode, l_learn, l_values, *l_adam) = loads

    barrier = pltpu.get_barrier_semaphore()

    def greet(device):
        pl.semaphore_signal(barrier, inc=1, device_id=device, device_id_type=MESH)

    for peer in (right, left, across):
        greet((g, peer))
    greet((grp_of(y, zh, 1 - core), t))
    for d in range(1, ZH):
        greet((grp_of(y, lax.rem(zh + d, ZH), core), t))
    for d in range(1, Y):
        greet((grp_of(lax.rem(y + d, Y), zh, core), t))
    l_cot.wait()
    turned = cot[...].T
    gathered[pl.ds(t * BLOCKS, BLOCKS)] = turned.reshape(BLOCKS, BLOCK, ROWS)

    pl.semaphore_wait(barrier, 3 + 1 + (ZH - 1) + (Y - 1))

    xl, xr, xx = tp_of(-1, 0), tp_of(1, 0), tp_of(2, 0)
    zo, zxl, zxr, zxx = tp_of(0, 1), tp_of(-1, 1), tp_of(1, 1), tp_of(2, 1)
    pieces = {
        "z0": (across, t, zo, 2, 3),
        "z1": (across, t, zo, 5, 3),
        "z2": (across, t, zo, 0, 2),
        "z3": (across, xl, zxl, 0, 2),
        "z4": (across, xr, zxr, 0, 2),
        "z5": (across, xx, zxx, 0, 2),
        "r0": (right, t, xl, 0, 4),
        "r1": (right, t, xl, 4, 4),
        "r2": (right, xl, xx, 0, 4),
        "r3": (right, zo, zxl, 2, 3),
        "r4": (right, zo, zxl, 5, 3),
        "r5": (right, zxl, zxx, 2, 3),
        "l0": (left, t, xr, 4, 4),
        "l1": (left, t, xr, 0, 4),
        "l2": (left, xr, xx, 4, 4),
        "l3": (left, zo, zxr, 5, 3),
        "l4": (left, zo, zxr, 2, 3),
        "l5": (left, zxr, zxx, 5, 3),
    }
    order = list(pieces)

    def piece(name, landed):
        peer, source, lands, first, count = pieces[name]
        blocks = gathered.at[pl.ds((lands if landed else source) * BLOCKS + first, count)]
        n = order.index(name)
        return remote(blocks, blocks, ag_send.at[n], ag_recv.at[n], (g, peer))

    def send(*names):
        for name in names:
            piece(name, False).start()

    def arrived(*names):
        for name in names:
            piece(name, True).wait_recv()

    send("z0", "r0", "l0")

    l_ids.wait()
    l_rewards.wait()
    group_at = lax.broadcasted_iota(jnp.int32, (GROUPS, ROWS), 0)
    id_row = jnp.concatenate([ids[k : k + 1, :] for k in range(ROWS // 128)], axis=1)
    reward_row = jnp.concatenate([rewards[k : k + 1, :] for k in range(ROWS // 128)], axis=1)
    member[...] = jnp.where(group_at == id_row, 1.0, 0.0).astype(bf16)
    high, middle, low = split_three(reward_row)
    rows = lax.broadcasted_iota(jnp.int32, (8, ROWS), 0)
    stack = jnp.where(
        rows == 0,
        high.astype(f32),
        jnp.where(rows == 1, middle.astype(f32), jnp.where(rows == 2, low.astype(f32), 1.0)),
    )
    totals_out[0] = dot(stack.astype(bf16), member[...], ((1,), (1,)))
    totals_of_core = remote(
        totals_out.at[0], totals_core, tot_send.at[0], tot_recv.at[0], (grp_of(y, zh, 1 - core), t)
    )
    totals_of_core.start()
    send("r1", "l1")

    totals_of_core.wait_recv()
    totals_out[1] = totals_out[0] + totals_core[...]

    def totals_over_z(d, landed):
        to, source = lax.rem(zh + d, ZH), lax.rem(zh - d + ZH, ZH)
        return remote(
            totals_out.at[1],
            totals_z.at[source if landed else zh],
            tot_send.at[d],
            tot_recv.at[d],
            (grp_of(y, to, core), t),
        )

    for d in range(1, ZH):
        totals_over_z(d, False).start()
    send("z1", "z2")

    total = totals_out[1]
    for d in range(1, ZH):
        totals_over_z(d, True).wait_recv()
        total = total + totals_z[lax.rem(zh - d + ZH, ZH)]
    totals_out[2] = total

    def totals_over_y(d, landed):
        to, source = lax.rem(y + d, Y), lax.rem(y - d + Y, Y)
        return remote(
            totals_out.at[2],
            totals_y.at[source if landed else y],
            tot_send.at[ZH + d],
            tot_recv.at[ZH + d],
            (grp_of(to, zh, core), t),
        )

    for d in range(1, Y):
        totals_over_y(d, False).start()

    l_decode.wait()
    decode_all[core, y] = decode_own[...].astype(f32)

    def decode_copy(d, landed):
        to, source = lax.rem(y + d, Y), lax.rem(y - d + Y, Y)
        block = decode_all.at[core, source if landed else y]
        return remote(block, block, dec_send.at[d], dec_recv.at[d], (grp_of(to, zh, core), t))

    for d in range(1, Y):
        decode_copy(d, False).start()

    arrived("r0")
    send("r2", "z3")
    arrived("l0")
    send("l2")

    for d in range(1, Y):
        totals_over_y(d, True).wait_recv()
        total = total + totals_y[lax.rem(y - d + Y, Y)]

    size = total[3:4]
    mean = jnp.where(
        size > 0.5, (total[0:1] + total[1:2] + total[2:3]) / jnp.maximum(size, 1.0), 0.0
    )
    high, middle, low = split_three(mean)
    rows = lax.broadcasted_iota(jnp.int32, (8, GROUPS), 0)
    stack = jnp.where(
        rows == 0,
        high.astype(f32),
        jnp.where(rows == 1, middle.astype(f32), jnp.where(rows == 2, low.astype(f32), 0.0)),
    )
    means = dot(stack.astype(bf16), member[...], ((1,), (0,)))
    advantage = (reward_row - (means[0:1] + means[1:2] + means[2:3])) / float(ROWS)
    l_learn.wait()
    for k in range(ROWS // 128):
        column = jnp.broadcast_to(advantage[:, k * 128 : (k + 1) * 128], (128, 128)).T
        scaled = learn[k * 128 : (k + 1) * 128, :].astype(f32) * jnp.concatenate(
            [column] * (WIDTH // 128), axis=1
        )
        learn[k * 128 : (k + 1) * 128, :] = scaled.astype(bf16)

    def head_of(step):
        x_off = jnp.where(
            jnp.logical_or(step == 1, step == 5),
            X - 1,
            jnp.where(
                jnp.logical_or(step == 2, step == 6),
                1,
                jnp.where(jnp.logical_or(step == 4, step == 7), 2, 0),
            ),
        )
        flip = jnp.where(jnp.logical_or(step == 3, step >= 5), 1, 0)
        return tp_of(x_off, flip)

    def core_copy(step):
        return remote(
            core_out.at[step],
            core_in.at[step],
            core_send.at[step],
            core_recv.at[step],
            (grp_of(y, zh, 1 - core), t),
        )

    def z_copy(step, d, landed):
        to, source = lax.rem(zh + d, ZH), lax.rem(zh - d + ZH, ZH)
        return remote(
            z_out.at[step, to],
            z_in.at[step, source if landed else zh],
            z_send.at[step * ZH + d],
            z_recv.at[step * ZH + d],
            (grp_of(y, to, core), t),
        )

    def y_copy(step, head):
        return remote(
            y_out.at[step], y_in.at[y], y_send.at[step], y_recv.at[y], (grp_of(head, zh, core), t)
        )

    def wide_copy(step, head):
        return remote(
            wide_out.at[step], wide_in.at[y], y_send.at[step], y_recv.at[y], (grp_of(head, zh, core), t)
        )

    star = jnp.where(y == head_of(0), 0, jnp.where(y == head_of(1), 1, 2))
    early = jnp.logical_or(star < 2, y == head_of(2))

    def over_z(step, block):
        kept[step] = block
        z_out[step] = block.astype(bf16).reshape(ZH, BLOCK, WIDTH)
        for d in range(1, ZH):
            z_copy(step, d, False).start()

    def z_total(step):
        total = kept[step, pl.ds(pl.multiple_of(zh * BLOCK, BLOCK), BLOCK)]
        for d in range(1, ZH):
            z_copy(step, d, True).wait_recv()
            total = total + z_in[step, lax.rem(zh - d + ZH, ZH)].astype(f32)
        return total

    def from_core(step):
        core_copy(step).wait_recv()
        over_z(step, kept[step] + core_in[step].astype(f32))

    def from_core_wide(step):
        core_copy(step).wait_recv()
        both = kept[step] + core_in[step].astype(f32)
        kept[step] = both
        head = head_of(step)

        @pl.when(head != y)
        def _():
            wide_out[step] = both.astype(bf16)
            wide_copy(step, head).start()

    def from_z(step, _):
        total = z_total(step)
        head = head_of(step)

        @pl.when(head == y)
        def _():
            own_sum[...] = total

        @pl.when(head != y)
        def _():
            y_out[step] = total.astype(bf16)
            y_copy(step, head).start()

        return 0

    def rows_of(step, parity):
        base = head_of(step) * BLOCKS
        return [gathered[base + 2 * k + parity] for k in range(ZH)]

    def multiply(heads):
        lhs = [rows_of(head, 1 - core) + rows_of(head, core) for head in heads]
        result = dot(jnp.concatenate(sum(lhs, []), axis=0), learn[...], ((1,), (0,)))
        for n, head in enumerate(heads):
            core_out[head] = result[2 * n * HALF : (2 * n + 1) * HALF].astype(bf16)
            core_copy(head).start()
            kept[head] = result[(2 * n + 1) * HALF : (2 * n + 2) * HALF]

    def one_step(step, _):
        @pl.when(step == 0)
        def _():
            arrived("r1")

        @pl.when(step == 1)
        def _():
            arrived("z0")
            send("r3")
            arrived("z1")
            send("l3", "r4", "l4")
            arrived("l1")
            send("z4")
            arrived("z2")

        @pl.when(step == 2)
        def _():
            arrived("r2", "l2")
            send("z5")

        @pl.when(step == 3)
        def _():
            arrived("r3", "l3")
            send("r5", "l5")
            arrived("r4", "z3", "l4", "z4")

        @pl.when(step == 4)
        def _():
            arrived("z5", "r5", "l5")

        single = jnp.logical_or(step == 2, step == 4)
        first = 2 * step - jnp.where(step >= 3, 1, 0)

        @pl.when(single)
        def _():
            multiply([first])

        @pl.when(jnp.logical_not(single))
        def _():
            multiply([first, first + 1])

        @pl.when(step == 1)
        def _():
            from_core_wide(0)
            from_core_wide(1)

        @pl.when(step == 2)
        def _():
            from_core_wide(2)
            from_core(3)

        @pl.when(step == 3)
        def _():
            from_core(4)
            from_z(3, 0)
            from_core(5)
            from_core(6)

        @pl.when(step == 4)
        def _():
            from_z(4, 0)

        return 0

    lax.fori_loop(0, 5, one_step, 0)
    from_core(TP - 1)

    def decode_across(at):
        block = decode_all.at[at]
        return remote(block, block, dec_send.at[0], dec_recv.at[0], (grp_of(y, zh, 1 - core), t))

    for d in range(1, Y):
        decode_copy(d, True).wait_recv()
    decode_across(core).start()

    lax.fori_loop(5, TP - 1, from_z, 0)

    @pl.when(early)
    def _():
        block = kept[star]
        for d in range(1, Y):
            source = lax.rem(y - d + Y, Y)
            landed = wide_in.at[source]
            remote(landed, landed, y_send.at[0], y_recv.at[source], (g, right)).wait_recv()
            block = block + wide_in[source].astype(f32)
        over_z(star, block)

    l_queries.wait()
    l_fresh.wait()
    l_keys.wait()
    scale = 1.0 / math.sqrt(HEAD_SIZE)
    tiles = queries[...].astype(f32)
    tiles = jnp.concatenate(
        [tiles[:, j * HEAD_SIZE : (j + 1) * HEAD_SIZE] for j in range(QUERIES)], axis=0
    )
    query_rows = tiles.astype(bf16)
    row_of = lax.broadcasted_iota(jnp.int32, (QUERIES * DECODE, SLOTS), 0) & (DECODE - 1)
    slot_of = lax.broadcasted_iota(jnp.int32, (QUERIES * DECODE, SLOTS), 1)
    scores = jnp.zeros((QUERIES * DECODE, SLOTS), f32)
    for r in range(DECODE):
        of_row = dot(query_rows, keys[r], ((1,), (1,))) * scale
        of_row = jnp.where(slot_of < lengths_ref[r], of_row, -jnp.inf)
        scores = jnp.where(row_of == r, of_row, scores)
    fresh_tiles = jnp.concatenate([fresh[...].astype(f32)] * QUERIES, axis=0)
    own_score = jnp.sum(tiles * fresh_tiles, axis=1, keepdims=True) * scale
    highest = jnp.maximum(jnp.max(scores, axis=1, keepdims=True), own_score)
    cache_exp = jnp.exp(scores - highest)
    own_exp = jnp.exp(own_score - highest)
    denominator = jnp.sum(cache_exp, axis=1, keepdims=True) + own_exp
    weights[...] = (cache_exp / denominator).astype(bf16)
    own_weight = (own_exp / denominator).astype(bf16).astype(f32)
    own_part[...] = jnp.broadcast_to(own_weight, (QUERIES * DECODE, HEAD_SIZE))

    from_z(TP - 1, 0)

    l_values.wait()
    row_at = lax.broadcasted_iota(jnp.int32, (QUERIES * DECODE, HEAD_SIZE), 0) & (DECODE - 1)
    cached = jnp.zeros((QUERIES * DECODE, HEAD_SIZE), f32)
    for r in range(DECODE):
        of_row = dot(weights[...], values[r], ((1,), (0,)))
        cached = jnp.where(row_at == r, of_row, cached)
    cache_part[...] = cached

    for owner in range(ZH):
        fresh_rows[owner * CORE + 1 - core] = jnp.zeros((BLOCK, WIDTH), bf16)

    @pl.when(early)
    def _():
        own_sum[...] = z_total(star)

    @pl.when(jnp.logical_not(early))
    def _():
        total = own_sum[...]
        for d in range(1, Y):
            source = lax.rem(y - d + Y, Y)
            landed = y_in.at[source]
            remote(landed, landed, y_send.at[0], y_recv.at[source], (g, right)).wait_recv()
            total = total + y_in[source].astype(f32)
        own_sum[...] = total

    for load in l_adam:
        load.wait()
    gradient = own_sum[...]

    updated, _, _ = optimizer_step(gradient, adam_in[0], adam_in[1], adam_in[2])

    mine = zh * CORE + core

    def row_copy(d, landed):
        to, source = lax.rem(zh + d, ZH), lax.rem(zh - d + ZH, ZH)
        block = fresh_rows.at[(source if landed else zh) * CORE + core]
        return remote(block, block, row_send.at[d], row_recv.at[d], (grp_of(y, to, core), t))

    fresh_rows[mine] = updated.astype(bf16)
    for d in range(1, ZH):
        row_copy(d, False).start()
    store = pltpu.make_async_copy(own_sum, gradient_hbm, store_sem.at[0])
    store.start()
    decode_across(1 - core).wait_recv()
    decode = decode_all[...].reshape(CORE * Y * DECODE, WIDTH).astype(bf16)
    for d in range(1, ZH):
        row_copy(d, True).wait_recv()

    part = dot(decode, fresh_rows[...].reshape(HEAD_SIZE, WIDTH), ((1,), (1,)))
    part_out[...] = part.reshape(CORE, Y, DECODE, HEAD_SIZE)

    def stays(row, of_core, peer):
        return jnp.logical_and(
            jnp.logical_and(y == t, row == y), jnp.logical_and(of_core == core, peer == t)
        )

    def part_copy(of_core, to):
        return remote(
            part_out.at[of_core, to],
            part_in.at[core, t],
            part_send.at[of_core * Y + to],
            part_recv.at[core * TP + t],
            (grp_of(to, zh, of_core), y),
        )

    for of_core in range(CORE):
        for to in range(Y):

            @pl.when(stays(to, of_core, t))
            def _():
                part_in[core, t] = part_out[of_core, to]

            @pl.when(jnp.logical_not(stays(to, of_core, t)))
            def _():
                part_copy(of_core, to).start()

    for of_core in range(CORE):
        for source in range(TP):

            @pl.when(jnp.logical_not(stays(y, of_core, source)))
            def _():
                landed = part_in.at[of_core, source]
                remote(
                    landed,
                    landed,
                    part_send.at[0],
                    part_recv.at[of_core * TP + source],
                    (grp_of(y, zh, 1 - core), t),
                ).wait_recv()

    new_values = jnp.sum(part_in[...].reshape(CORE * TP, DECODE, HEAD_SIZE), axis=0)
    new_values = new_values.astype(bf16).astype(f32)
    outcome = cache_part[...] + own_part[...] * jnp.concatenate([new_values] * QUERIES, axis=0)
    attended[...] = jnp.concatenate(
        [outcome[j * DECODE : (j + 1) * DECODE] for j in range(QUERIES)], axis=1
    )
    result_store = pltpu.make_async_copy(attended, attended_hbm, store_sem.at[1])
    result_store.start()

    for name in order:
        piece(name, False).wait_send()
    totals_of_core.wait_send()
    for d in range(1, ZH):
        totals_over_z(d, False).wait_send()
        row_copy(d, False).wait_send()
    for d in range(1, Y):
        totals_over_y(d, False).wait_send()
        decode_copy(d, False).wait_send()
    decode_across(core).wait_send()
    for step in range(TP):
        core_copy(step).wait_send()
        head = head_of(step)
        if step >= WIDE:
            for d in range(1, ZH):
                z_copy(step, d, False).wait_send()

        @pl.when(head != y)
        def _():
            (y_copy if step >= WIDE else wide_copy)(step, head).wait_send()

    @pl.when(early)
    def _():
        for d in range(1, ZH):
            z_copy(star, d, False).wait_send()

    for of_core in range(CORE):
        for to in range(Y):

            @pl.when(jnp.logical_not(stays(to, of_core, t)))
            def _():
                part_copy(of_core, to).wait_send()

    store.wait()
    result_store.wait()


def finish_kernel(gradient, master, one, two, attended, new_master, new_one, new_two, rounded):
    new_master[...], new_one[...], new_two[...] = optimizer_step(
        gradient[...], master[...], one[...], two[...]
    )
    rounded[...] = attended[...].astype(bf16)


def per_device(
    learn_rows,
    cot_values,
    rewards,
    group_ids,
    master,
    moment_one,
    moment_two,
    decode_rows,
    queries,
    fresh_keys,
    stored_keys,
    stored_values,
    cache_lengths,
):
    dma = pltpu.SemaphoreType.DMA
    shard = jax.ShapeDtypeStruct((BLOCK, WIDTH), f32)
    heads = QUERIES * HEAD_SIZE
    scratch = [
        ((ROWS, HEAD_SIZE), bf16),
        ((ROWS, WIDTH), bf16),
        ((ROWS // 128, 128), f32),
        ((ROWS // 128, 128), jnp.int32),
        ((3, BLOCK, WIDTH), f32),
        ((DECODE, WIDTH), bf16),
        ((DECODE, heads), bf16),
        ((DECODE, HEAD_SIZE), bf16),
        ((DECODE, SLOTS, HEAD_SIZE), bf16),
        ((DECODE, SLOTS, HEAD_SIZE), bf16),
        ((DECODE, heads), f32),
        ((TP * BLOCKS, BLOCK, ROWS), bf16),
        ((GROUPS, ROWS), bf16),
        ((3, 8, GROUPS), f32),
        ((8, GROUPS), f32),
        ((ZH, 8, GROUPS), f32),
        ((Y, 8, GROUPS), f32),
        ((CORE, Y, DECODE, WIDTH), f32),
        ((QUERIES * DECODE, SLOTS), bf16),
        ((QUERIES * DECODE, HEAD_SIZE), f32),
        ((QUERIES * DECODE, HEAD_SIZE), f32),
        ((TP, HALF, WIDTH), f32),
        ((TP, HALF, WIDTH), bf16),
        ((TP, HALF, WIDTH), bf16),
        ((TP, ZH, BLOCK, WIDTH), bf16),
        ((TP, ZH, BLOCK, WIDTH), bf16),
        ((TP, BLOCK, WIDTH), bf16),
        ((Y, BLOCK, WIDTH), bf16),
        ((WIDE, HALF, WIDTH), bf16),
        ((Y, HALF, WIDTH), bf16),
        ((BLOCK, WIDTH), f32),
        ((ZH * CORE, BLOCK, WIDTH), bf16),
        ((CORE, Y, DECODE, HEAD_SIZE), f32),
        ((CORE, TP, DECODE, HEAD_SIZE), f32),
    ]
    semaphores = [12, 2, 18, 18, TP, TP, TP * ZH, TP * ZH, TP, Y, ZH, ZH, CORE * Y, CORE * TP, ZH + Y, ZH + Y, Y, Y]
    hbm = pl.BlockSpec(memory_space=pltpu.HBM)
    gradient, attended = pl.pallas_call(
        kernel,
        out_shape=(shard, jax.ShapeDtypeStruct((DECODE, heads), f32)),
        in_specs=[hbm] * 12 + [pl.BlockSpec(memory_space=pltpu.SMEM)],
        out_specs=[hbm] * 2,
        scratch_shapes=[pltpu.VMEM(shape, kind) for shape, kind in scratch]
        + [dma((n,)) for n in semaphores],
        compiler_params=pltpu.CompilerParams(
            collective_id=0, has_side_effects=True, vmem_limit_bytes=60 * 1024 * 1024
        ),
    )(
        cot_values,
        learn_rows,
        rewards.reshape(ROWS // 128, 128),
        group_ids.reshape(ROWS // 128, 128),
        master,
        moment_one,
        moment_two,
        decode_rows,
        queries,
        fresh_keys,
        stored_keys,
        stored_values,
        cache_lengths,
    )
    return pl.pallas_call(
        finish_kernel,
        out_shape=(shard, shard, shard, jax.ShapeDtypeStruct((DECODE, heads), bf16)),
    )(gradient, master, moment_one, moment_two, attended)


def solution(mesh):
    shards, rows = P("grp", "tp"), P("grp")
    cache = P("grp", None, "tp")
    in_specs = (
        shards,
        shards,
        rows,
        rows,
        shards,
        shards,
        shards,
        P("grp", None),
        shards,
        shards,
        cache,
        cache,
        rows,
    )
    return jax.shard_map(
        per_device, mesh=mesh, in_specs=in_specs, out_specs=(shards,) * 4, check_vma=False
    )
```

```python
import math

import jax
import jax.numpy as jnp
from jax import lax
from jax.experimental import pallas as pl
from jax.experimental.pallas import tpu as pltpu
from jax.sharding import PartitionSpec as P

HEAD_SIZE = 128
QUERIES = 8
ROWS = 1536
WIDTH = 640
GROUPS = 256
SLOTS = 256
DECODE = 8
Y, ZH, CORE, X, ZL = 8, 4, 2, 4, 2
TP = X * ZL
BLOCKS = 8
BLOCK = 16
HALF = 64
WIDE = 3
FAR_Z = (2, 1, 3)
FAR_Y = (4, 3, 5, 2, 6, 1, 7)

beta_one = 0.9
beta_two = 0.95
learning_rate = 0.001
weight_decay = 0.1
adam_epsilon = 1e-08
step_count = 2.0

MESH = pl.DeviceIdType.MESH
bf16, f32 = jnp.bfloat16, jnp.float32


def split_three(value):
    high = value.astype(bf16)
    rest = value - high.astype(f32)
    middle = rest.astype(bf16)
    low = (rest - middle.astype(f32)).astype(bf16)
    return high, middle, low


def optimizer_step(gradient, master, moment_one, moment_two):
    first = beta_one * moment_one + (1.0 - beta_one) * gradient
    second = beta_two * moment_two + (1.0 - beta_two) * gradient * gradient
    first_hat = first / (1.0 - beta_one**step_count)
    second_hat = second / (1.0 - beta_two**step_count)
    updated = master - learning_rate * (
        first_hat / (jnp.sqrt(second_hat) + adam_epsilon) + weight_decay * master
    )
    return updated, first, second


def dot(a, b, dims):
    return lax.dot_general(a, b, (dims, ((), ())), preferred_element_type=f32)


def kernel(
    cot_hbm,
    learn_hbm,
    rewards_hbm,
    ids_hbm,
    master_hbm,
    one_hbm,
    two_hbm,
    decode_hbm,
    queries_hbm,
    fresh_hbm,
    keys_hbm,
    values_hbm,
    lengths_ref,
    gradient_hbm,
    attended_hbm,
    cot,
    learn,
    rewards,
    ids,
    adam_in,
    decode_own,
    queries,
    fresh,
    keys,
    values,
    attended,
    gathered,
    member,
    totals_out,
    totals_core,
    totals_z,
    totals_y,
    decode_all,
    weights,
    cache_part,
    own_part,
    kept,
    core_out,
    core_in,
    z_out,
    z_in,
    y_out,
    y_in,
    wide_out,
    wide_in,
    own_sum,
    fresh_rows,
    part_out,
    part_in,
    load_sem,
    store_sem,
    ag_send,
    ag_recv,
    core_send,
    core_recv,
    z_send,
    z_recv,
    y_send,
    y_recv,
    row_send,
    row_recv,
    part_send,
    part_recv,
    tot_send,
    tot_recv,
    dec_send,
    dec_recv,
):
    g, t = lax.axis_index("grp"), lax.axis_index("tp")
    y, zh, core = g // (ZH * CORE), lax.rem(g // CORE, ZH), lax.rem(g, CORE)
    x, zl = t // ZL, lax.rem(t, ZL)

    def grp_of(y_at, zh_at, core_at):
        return (y_at * ZH + zh_at) * CORE + core_at

    def tp_of(x_off, flip):
        return lax.rem(x + x_off + X, X) * ZL + lax.rem(zl + flip, ZL)

    right, left, across = tp_of(1, 0), tp_of(-1, 0), tp_of(0, 1)

    def remote(src, dst, send, recv, device):
        return pltpu.make_async_remote_copy(
            src_ref=src,
            dst_ref=dst,
            send_sem=send,
            recv_sem=recv,
            device_id=device,
            device_id_type=MESH,
        )

    loads = [
        (cot_hbm, cot),
        (ids_hbm, ids),
        (rewards_hbm, rewards),
        (queries_hbm, queries),
        (fresh_hbm, fresh),
        (keys_hbm, keys),
        (decode_hbm.at[:, pl.ds(pl.multiple_of(t * WIDTH, 128), WIDTH)], decode_own),
        (learn_hbm, learn),
        (values_hbm, values),
        (master_hbm, adam_in.at[0]),
        (one_hbm, adam_in.at[1]),
        (two_hbm, adam_in.at[2]),
    ]
    loads = [pltpu.make_async_copy(src, dst, load_sem.at[i]) for i, (src, dst) in enumerate(loads)]
    for load in loads[:3]:
        load.start()
    (l_cot, l_ids, l_rewards, l_queries, l_fresh, l_keys, l_decode, l_learn, l_values, *l_adam) = loads

    barrier = pltpu.get_barrier_semaphore()

    def greet(device):
        pl.semaphore_signal(barrier, inc=1, device_id=device, device_id_type=MESH)

    for peer in (right, left, across):
        greet((g, peer))
    greet((grp_of(y, zh, 1 - core), t))
    for d in range(1, ZH):
        greet((grp_of(y, lax.rem(zh + d, ZH), core), t))
    for d in range(1, Y):
        greet((grp_of(lax.rem(y + d, Y), zh, core), t))
    l_cot.wait()
    turned = cot[...].T
    gathered[pl.ds(t * BLOCKS, BLOCKS)] = turned.reshape(BLOCKS, BLOCK, ROWS)

    pl.semaphore_wait(barrier, 3 + 1 + (ZH - 1) + (Y - 1))

    xl, xr, xx = tp_of(-1, 0), tp_of(1, 0), tp_of(2, 0)
    zo, zxl, zxr, zxx = tp_of(0, 1), tp_of(-1, 1), tp_of(1, 1), tp_of(2, 1)
    pieces = {
        "z0": (across, t, zo, 2, 3),
        "z1": (across, t, zo, 5, 3),
        "z2": (across, t, zo, 0, 2),
        "z3": (across, xl, zxl, 0, 2),
        "z4": (across, xr, zxr, 0, 2),
        "z5": (across, xx, zxx, 0, 2),
        "r0": (right, t, xl, 0, 4),
        "r1": (right, t, xl, 4, 4),
        "r2": (right, xl, xx, 0, 4),
        "r3": (right, zo, zxl, 2, 3),
        "r4": (right, zo, zxl, 5, 3),
        "r5": (right, zxl, zxx, 2, 3),
        "l0": (left, t, xr, 4, 4),
        "l1": (left, t, xr, 0, 4),
        "l2": (left, xr, xx, 4, 4),
        "l3": (left, zo, zxr, 5, 3),
        "l4": (left, zo, zxr, 2, 3),
        "l5": (left, zxr, zxx, 5, 3),
    }
    order = list(pieces)

    def piece(name, landed):
        peer, source, lands, first, count = pieces[name]
        blocks = gathered.at[pl.ds((lands if landed else source) * BLOCKS + first, count)]
        n = order.index(name)
        return remote(blocks, blocks, ag_send.at[n], ag_recv.at[n], (g, peer))

    def send(*names):
        for name in names:
            piece(name, False).start()

    def arrived(*names):
        for name in names:
            piece(name, True).wait_recv()

    send("z0", "r0", "l0")
    for load in loads[3:]:
        load.start()

    l_ids.wait()
    l_rewards.wait()
    group_at = lax.broadcasted_iota(jnp.int32, (GROUPS, ROWS), 0)
    id_row = jnp.concatenate([ids[k : k + 1, :] for k in range(ROWS // 128)], axis=1)
    reward_row = jnp.concatenate([rewards[k : k + 1, :] for k in range(ROWS // 128)], axis=1)
    member[...] = jnp.where(group_at == id_row, 1.0, 0.0).astype(bf16)
    high, middle, low = split_three(reward_row)
    rows = lax.broadcasted_iota(jnp.int32, (8, ROWS), 0)
    stack = jnp.where(
        rows == 0,
        high.astype(f32),
        jnp.where(rows == 1, middle.astype(f32), jnp.where(rows == 2, low.astype(f32), 1.0)),
    )
    totals_out[0] = dot(stack.astype(bf16), member[...], ((1,), (1,)))
    totals_of_core = remote(
        totals_out.at[0], totals_core, tot_send.at[0], tot_recv.at[0], (grp_of(y, zh, 1 - core), t)
    )
    totals_of_core.start()
    send("r1", "l1")

    totals_of_core.wait_recv()
    totals_out[1] = totals_out[0] + totals_core[...]

    def totals_over_z(d, landed):
        to, source = lax.rem(zh + d, ZH), lax.rem(zh - d + ZH, ZH)
        return remote(
            totals_out.at[1],
            totals_z.at[source if landed else zh],
            tot_send.at[d],
            tot_recv.at[d],
            (grp_of(y, to, core), t),
        )

    for d in FAR_Z:
        totals_over_z(d, False).start()
    send("z1", "z2")

    total = totals_out[1]
    for d in range(1, ZH):
        totals_over_z(d, True).wait_recv()
        total = total + totals_z[lax.rem(zh - d + ZH, ZH)]
    totals_out[2] = total

    def totals_over_y(d, landed):
        to, source = lax.rem(y + d, Y), lax.rem(y - d + Y, Y)
        return remote(
            totals_out.at[2],
            totals_y.at[source if landed else y],
            tot_send.at[ZH + d],
            tot_recv.at[ZH + d],
            (grp_of(to, zh, core), t),
        )

    for d in FAR_Y:
        totals_over_y(d, False).start()

    l_decode.wait()
    decode_all[core, y] = decode_own[...].astype(f32)

    def decode_copy(d, landed):
        to, source = lax.rem(y + d, Y), lax.rem(y - d + Y, Y)
        block = decode_all.at[core, source if landed else y]
        return remote(block, block, dec_send.at[d], dec_recv.at[d], (grp_of(to, zh, core), t))

    for d in range(1, Y):
        decode_copy(d, False).start()

    arrived("r0")
    send("r2", "z3")
    arrived("l0")
    send("l2")

    for d in range(1, Y):
        totals_over_y(d, True).wait_recv()
        total = total + totals_y[lax.rem(y - d + Y, Y)]

    size = total[3:4]
    mean = jnp.where(
        size > 0.5, (total[0:1] + total[1:2] + total[2:3]) / jnp.maximum(size, 1.0), 0.0
    )
    high, middle, low = split_three(mean)
    rows = lax.broadcasted_iota(jnp.int32, (8, GROUPS), 0)
    stack = jnp.where(
        rows == 0,
        high.astype(f32),
        jnp.where(rows == 1, middle.astype(f32), jnp.where(rows == 2, low.astype(f32), 0.0)),
    )
    means = dot(stack.astype(bf16), member[...], ((1,), (0,)))
    advantage = (reward_row - (means[0:1] + means[1:2] + means[2:3])) / float(ROWS)
    l_learn.wait()
    for k in range(ROWS // 128):
        column = jnp.broadcast_to(advantage[:, k * 128 : (k + 1) * 128], (128, 128)).T
        scaled = learn[k * 128 : (k + 1) * 128, :].astype(f32) * jnp.concatenate(
            [column] * (WIDTH // 128), axis=1
        )
        learn[k * 128 : (k + 1) * 128, :] = scaled.astype(bf16)

    def head_of(step):
        x_off = jnp.where(
            jnp.logical_or(step == 1, step == 5),
            X - 1,
            jnp.where(
                jnp.logical_or(step == 2, step == 6),
                1,
                jnp.where(jnp.logical_or(step == 4, step == 7), 2, 0),
            ),
        )
        flip = jnp.where(jnp.logical_or(step == 3, step >= 5), 1, 0)
        return tp_of(x_off, flip)

    def core_copy(step):
        return remote(
            core_out.at[step],
            core_in.at[step],
            core_send.at[step],
            core_recv.at[step],
            (grp_of(y, zh, 1 - core), t),
        )

    def z_copy(step, d, landed):
        to, source = lax.rem(zh + d, ZH), lax.rem(zh - d + ZH, ZH)
        return remote(
            z_out.at[step, to],
            z_in.at[step, source if landed else zh],
            z_send.at[step * ZH + d],
            z_recv.at[step * ZH + d],
            (grp_of(y, to, core), t),
        )

    def y_copy(step, head):
        return remote(
            y_out.at[step], y_in.at[y], y_send.at[step], y_recv.at[y], (grp_of(head, zh, core), t)
        )

    def wide_copy(step, head):
        return remote(
            wide_out.at[step], wide_in.at[y], y_send.at[step], y_recv.at[y], (grp_of(head, zh, core), t)
        )

    star = jnp.where(y == head_of(0), 0, jnp.where(y == head_of(1), 1, 2))
    early = jnp.logical_or(star < 2, y == head_of(2))

    def over_z(step, block):
        kept[step] = block
        z_out[step] = block.astype(bf16).reshape(ZH, BLOCK, WIDTH)
        for d in FAR_Z:
            z_copy(step, d, False).start()

    def z_total(step):
        total = kept[step, pl.ds(pl.multiple_of(zh * BLOCK, BLOCK), BLOCK)]
        for d in range(1, ZH):
            z_copy(step, d, True).wait_recv()
            total = total + z_in[step, lax.rem(zh - d + ZH, ZH)].astype(f32)
        return total

    def from_core(step):
        core_copy(step).wait_recv()
        over_z(step, kept[step] + core_in[step].astype(f32))

    def from_core_wide(step):
        core_copy(step).wait_recv()
        both = kept[step] + core_in[step].astype(f32)
        kept[step] = both
        head = head_of(step)

        @pl.when(head != y)
        def _():
            wide_out[step] = both.astype(bf16)
            wide_copy(step, head).start()

    def from_z(step, _):
        total = z_total(step)
        head = head_of(step)

        @pl.when(head == y)
        def _():
            own_sum[...] = total

        @pl.when(head != y)
        def _():
            y_out[step] = total.astype(bf16)
            y_copy(step, head).start()

        return 0

    def rows_of(step, parity):
        base = head_of(step) * BLOCKS
        return [gathered[base + 2 * k + parity] for k in range(ZH)]

    def multiply(heads):
        lhs = [rows_of(head, 1 - core) + rows_of(head, core) for head in heads]
        result = dot(jnp.concatenate(sum(lhs, []), axis=0), learn[...], ((1,), (0,)))
        for n, head in enumerate(heads):
            core_out[head] = result[2 * n * HALF : (2 * n + 1) * HALF].astype(bf16)
            core_copy(head).start()
            kept[head] = result[(2 * n + 1) * HALF : (2 * n + 2) * HALF]

    def one_step(step, _):
        @pl.when(step == 0)
        def _():
            arrived("r1")

        @pl.when(step == 1)
        def _():
            arrived("z0")
            send("r3")
            arrived("z1")
            send("l3", "r4", "l4")
            arrived("l1")
            send("z4")
            arrived("z2")

        @pl.when(step == 2)
        def _():
            arrived("r2", "l2")
            send("z5")

        @pl.when(step == 3)
        def _():
            arrived("r3", "l3")
            send("r5", "l5")
            arrived("r4", "z3", "l4", "z4")

        @pl.when(step == 4)
        def _():
            arrived("z5", "r5", "l5")

        single = jnp.logical_or(step == 2, step == 4)
        first = 2 * step - jnp.where(step >= 3, 1, 0)

        @pl.when(single)
        def _():
            multiply([first])

        @pl.when(jnp.logical_not(single))
        def _():
            multiply([first, first + 1])

        @pl.when(step == 1)
        def _():
            from_core_wide(0)
            from_core_wide(1)

        @pl.when(step == 2)
        def _():
            from_core_wide(2)
            from_core(3)

        @pl.when(step == 3)
        def _():
            from_core(4)
            from_z(3, 0)
            from_core(5)
            from_core(6)

        @pl.when(step == 4)
        def _():
            from_z(4, 0)

        return 0

    lax.fori_loop(0, 5, one_step, 0)
    from_core(TP - 1)

    def decode_across(at):
        block = decode_all.at[at]
        return remote(block, block, dec_send.at[0], dec_recv.at[0], (grp_of(y, zh, 1 - core), t))

    for d in range(1, Y):
        decode_copy(d, True).wait_recv()
    decode_across(core).start()

    lax.fori_loop(5, TP - 1, from_z, 0)

    @pl.when(early)
    def _():
        block = kept[star]
        for d in range(1, Y):
            source = lax.rem(y - d + Y, Y)
            landed = wide_in.at[source]
            remote(landed, landed, y_send.at[0], y_recv.at[source], (g, right)).wait_recv()
            block = block + wide_in[source].astype(f32)
        over_z(star, block)

    l_queries.wait()
    l_fresh.wait()
    l_keys.wait()
    scale = 1.0 / math.sqrt(HEAD_SIZE)
    tiles = queries[...].astype(f32)
    tiles = jnp.concatenate(
        [tiles[:, j * HEAD_SIZE : (j + 1) * HEAD_SIZE] for j in range(QUERIES)], axis=0
    )
    query_rows = tiles.astype(bf16)
    row_of = lax.broadcasted_iota(jnp.int32, (QUERIES * DECODE, SLOTS), 0) & (DECODE - 1)
    slot_of = lax.broadcasted_iota(jnp.int32, (QUERIES * DECODE, SLOTS), 1)
    scores = jnp.zeros((QUERIES * DECODE, SLOTS), f32)
    for r in range(DECODE):
        of_row = dot(query_rows, keys[r], ((1,), (1,))) * scale
        of_row = jnp.where(slot_of < lengths_ref[r], of_row, -jnp.inf)
        scores = jnp.where(row_of == r, of_row, scores)
    fresh_tiles = jnp.concatenate([fresh[...].astype(f32)] * QUERIES, axis=0)
    own_score = jnp.sum(tiles * fresh_tiles, axis=1, keepdims=True) * scale
    highest = jnp.maximum(jnp.max(scores, axis=1, keepdims=True), own_score)
    cache_exp = jnp.exp(scores - highest)
    own_exp = jnp.exp(own_score - highest)
    denominator = jnp.sum(cache_exp, axis=1, keepdims=True) + own_exp
    weights[...] = (cache_exp / denominator).astype(bf16)
    own_weight = (own_exp / denominator).astype(bf16).astype(f32)
    own_part[...] = jnp.broadcast_to(own_weight, (QUERIES * DECODE, HEAD_SIZE))

    from_z(TP - 1, 0)

    l_values.wait()
    row_at = lax.broadcasted_iota(jnp.int32, (QUERIES * DECODE, HEAD_SIZE), 0) & (DECODE - 1)
    cached = jnp.zeros((QUERIES * DECODE, HEAD_SIZE), f32)
    for r in range(DECODE):
        of_row = dot(weights[...], values[r], ((1,), (0,)))
        cached = jnp.where(row_at == r, of_row, cached)
    cache_part[...] = cached

    for owner in range(ZH):
        fresh_rows[owner * CORE + 1 - core] = jnp.zeros((BLOCK, WIDTH), bf16)

    @pl.when(early)
    def _():
        own_sum[...] = z_total(star)

    @pl.when(jnp.logical_not(early))
    def _():
        total = own_sum[...]
        for d in range(1, Y):
            source = lax.rem(y - d + Y, Y)
            landed = y_in.at[source]
            remote(landed, landed, y_send.at[0], y_recv.at[source], (g, right)).wait_recv()
            total = total + y_in[source].astype(f32)
        own_sum[...] = total

    for load in l_adam:
        load.wait()
    gradient = own_sum[...]

    updated, _, _ = optimizer_step(gradient, adam_in[0], adam_in[1], adam_in[2])

    mine = zh * CORE + core

    def row_copy(d, landed):
        to, source = lax.rem(zh + d, ZH), lax.rem(zh - d + ZH, ZH)
        block = fresh_rows.at[(source if landed else zh) * CORE + core]
        return remote(block, block, row_send.at[d], row_recv.at[d], (grp_of(y, to, core), t))

    fresh_rows[mine] = updated.astype(bf16)
    for d in FAR_Z:
        row_copy(d, False).start()
    store = pltpu.make_async_copy(own_sum, gradient_hbm, store_sem.at[0])
    store.start()
    decode_across(1 - core).wait_recv()
    decode = decode_all[...].reshape(CORE * Y * DECODE, WIDTH).astype(bf16)

    for name in order:
        piece(name, False).wait_send()
    totals_of_core.wait_send()
    for d in range(1, ZH):
        totals_over_z(d, False).wait_send()
    for d in range(1, Y):
        totals_over_y(d, False).wait_send()
        decode_copy(d, False).wait_send()
    decode_across(core).wait_send()
    for step in range(TP):
        core_copy(step).wait_send()
        head = head_of(step)
        if step >= WIDE:
            for d in range(1, ZH):
                z_copy(step, d, False).wait_send()

        @pl.when(head != y)
        def _():
            (y_copy if step >= WIDE else wide_copy)(step, head).wait_send()

    @pl.when(early)
    def _():
        for d in range(1, ZH):
            z_copy(star, d, False).wait_send()

    for d in range(1, ZH):
        row_copy(d, True).wait_recv()

    part = dot(decode, fresh_rows[...].reshape(HEAD_SIZE, WIDTH), ((1,), (1,)))
    part_out[...] = part.reshape(CORE, Y, DECODE, HEAD_SIZE)

    def part_copy(of_core, d):
        to = lax.rem(y + d, Y)
        return remote(
            part_out.at[of_core, to],
            part_in.at[core, t],
            part_send.at[of_core * Y + to],
            part_recv.at[core * TP + t],
            (grp_of(to, zh, of_core), y),
        )

    for d in FAR_Y:
        part_copy(core, d).start()
        part_copy(1 - core, d).start()
    part_copy(1 - core, 0).start()

    @pl.when(t == y)
    def _():
        part_in[core, t] = part_out[core, y]

    @pl.when(t != y)
    def _():
        part_copy(core, 0).start()

    def part_arrived(of_core, d):
        source = lax.rem(t + d, TP)
        landed = part_in.at[of_core, source]
        remote(
            landed,
            landed,
            part_send.at[0],
            part_recv.at[of_core * TP + source],
            (grp_of(y, zh, 1 - core), t),
        ).wait_recv()

    for d in range(1, TP):
        part_arrived(core, d)
        part_arrived(1 - core, d)
    part_arrived(1 - core, 0)

    @pl.when(t != y)
    def _():
        part_arrived(core, 0)

    new_values = jnp.sum(part_in[...].reshape(CORE * TP, DECODE, HEAD_SIZE), axis=0)
    new_values = new_values.astype(bf16).astype(f32)
    outcome = cache_part[...] + own_part[...] * jnp.concatenate([new_values] * QUERIES, axis=0)
    attended[...] = jnp.concatenate(
        [outcome[j * DECODE : (j + 1) * DECODE] for j in range(QUERIES)], axis=1
    )
    result_store = pltpu.make_async_copy(attended, attended_hbm, store_sem.at[1])
    result_store.start()

    for d in range(1, ZH):
        row_copy(d, False).wait_send()
    for d in range(Y):
        part_copy(1 - core, d).wait_send()
    for d in range(1, Y):
        part_copy(core, d).wait_send()

    @pl.when(t != y)
    def _():
        part_copy(core, 0).wait_send()

    store.wait()
    result_store.wait()


def finish_kernel(gradient, master, one, two, attended, new_master, new_one, new_two, rounded):
    new_master[...], new_one[...], new_two[...] = optimizer_step(
        gradient[...], master[...], one[...], two[...]
    )
    rounded[...] = attended[...].astype(bf16)


def per_device(
    learn_rows,
    cot_values,
    rewards,
    group_ids,
    master,
    moment_one,
    moment_two,
    decode_rows,
    queries,
    fresh_keys,
    stored_keys,
    stored_values,
    cache_lengths,
):
    dma = pltpu.SemaphoreType.DMA
    shard = jax.ShapeDtypeStruct((BLOCK, WIDTH), f32)
    heads = QUERIES * HEAD_SIZE
    scratch = [
        ((ROWS, HEAD_SIZE), bf16),
        ((ROWS, WIDTH), bf16),
        ((ROWS // 128, 128), f32),
        ((ROWS // 128, 128), jnp.int32),
        ((3, BLOCK, WIDTH), f32),
        ((DECODE, WIDTH), bf16),
        ((DECODE, heads), bf16),
        ((DECODE, HEAD_SIZE), bf16),
        ((DECODE, SLOTS, HEAD_SIZE), bf16),
        ((DECODE, SLOTS, HEAD_SIZE), bf16),
        ((DECODE, heads), f32),
        ((TP * BLOCKS, BLOCK, ROWS), bf16),
        ((GROUPS, ROWS), bf16),
        ((3, 8, GROUPS), f32),
        ((8, GROUPS), f32),
        ((ZH, 8, GROUPS), f32),
        ((Y, 8, GROUPS), f32),
        ((CORE, Y, DECODE, WIDTH), f32),
        ((QUERIES * DECODE, SLOTS), bf16),
        ((QUERIES * DECODE, HEAD_SIZE), f32),
        ((QUERIES * DECODE, HEAD_SIZE), f32),
        ((TP, HALF, WIDTH), f32),
        ((TP, HALF, WIDTH), bf16),
        ((TP, HALF, WIDTH), bf16),
        ((TP, ZH, BLOCK, WIDTH), bf16),
        ((TP, ZH, BLOCK, WIDTH), bf16),
        ((TP, BLOCK, WIDTH), bf16),
        ((Y, BLOCK, WIDTH), bf16),
        ((WIDE, HALF, WIDTH), bf16),
        ((Y, HALF, WIDTH), bf16),
        ((BLOCK, WIDTH), f32),
        ((ZH * CORE, BLOCK, WIDTH), bf16),
        ((CORE, Y, DECODE, HEAD_SIZE), f32),
        ((CORE, TP, DECODE, HEAD_SIZE), f32),
    ]
    semaphores = [12, 2, 18, 18, TP, TP, TP * ZH, TP * ZH, TP, Y, ZH, ZH, CORE * Y, CORE * TP, ZH + Y, ZH + Y, Y, Y]
    hbm = pl.BlockSpec(memory_space=pltpu.HBM)
    gradient, attended = pl.pallas_call(
        kernel,
        out_shape=(shard, jax.ShapeDtypeStruct((DECODE, heads), f32)),
        in_specs=[hbm] * 12 + [pl.BlockSpec(memory_space=pltpu.SMEM)],
        out_specs=[hbm] * 2,
        scratch_shapes=[pltpu.VMEM(shape, kind) for shape, kind in scratch]
        + [dma((n,)) for n in semaphores],
        compiler_params=pltpu.CompilerParams(
            collective_id=0, has_side_effects=True, vmem_limit_bytes=60 * 1024 * 1024
        ),
    )(
        cot_values,
        learn_rows,
        rewards.reshape(ROWS // 128, 128),
        group_ids.reshape(ROWS // 128, 128),
        master,
        moment_one,
        moment_two,
        decode_rows,
        queries,
        fresh_keys,
        stored_keys,
        stored_values,
        cache_lengths,
    )
    return pl.pallas_call(
        finish_kernel,
        out_shape=(shard, shard, shard, jax.ShapeDtypeStruct((DECODE, heads), bf16)),
    )(gradient, master, moment_one, moment_two, attended)


def solution(mesh):
    shards, rows = P("grp", "tp"), P("grp")
    cache = P("grp", None, "tp")
    in_specs = (
        shards,
        shards,
        rows,
        rows,
        shards,
        shards,
        shards,
        P("grp", None),
        shards,
        shards,
        cache,
        cache,
        rows,
    )
    return jax.shard_map(
        per_device, mesh=mesh, in_specs=in_specs, out_specs=(shards,) * 4, check_vma=False
    )
```

```python
import math

import jax
import jax.numpy as jnp
from jax import lax
from jax.experimental import pallas as pl
from jax.experimental.pallas import tpu as pltpu
from jax.sharding import PartitionSpec as P

HEAD_SIZE = 128
QUERIES = 8
ROWS = 1536
WIDTH = 640
GROUPS = 256
SLOTS = 256
DECODE = 8
Y, ZH, CORE, X, ZL = 8, 4, 2, 4, 2
TP = X * ZL
BLOCKS = 8
BLOCK = 16
HALF = 64
WIDE = 3
FAR_Z = (2, 1, 3)
FAR_Y = (4, 3, 5, 2, 6, 1, 7)

beta_one = 0.9
beta_two = 0.95
learning_rate = 0.001
weight_decay = 0.1
adam_epsilon = 1e-08
step_count = 2.0

MESH = pl.DeviceIdType.MESH
bf16, f32 = jnp.bfloat16, jnp.float32


def split_three(value):
    high = value.astype(bf16)
    rest = value - high.astype(f32)
    middle = rest.astype(bf16)
    low = (rest - middle.astype(f32)).astype(bf16)
    return high, middle, low


def optimizer_step(gradient, master, moment_one, moment_two):
    first = beta_one * moment_one + (1.0 - beta_one) * gradient
    second = beta_two * moment_two + (1.0 - beta_two) * gradient * gradient
    first_hat = first / (1.0 - beta_one**step_count)
    second_hat = second / (1.0 - beta_two**step_count)
    updated = master - learning_rate * (
        first_hat / (jnp.sqrt(second_hat) + adam_epsilon) + weight_decay * master
    )
    return updated, first, second


def dot(a, b, dims):
    return lax.dot_general(a, b, (dims, ((), ())), preferred_element_type=f32)


def kernel(
    cot_hbm,
    learn_hbm,
    rewards_hbm,
    ids_hbm,
    master_hbm,
    one_hbm,
    two_hbm,
    decode_hbm,
    queries_hbm,
    fresh_hbm,
    keys_hbm,
    values_hbm,
    lengths_ref,
    gradient_hbm,
    attended_hbm,
    cot,
    learn,
    rewards,
    ids,
    adam_in,
    decode_own,
    queries,
    fresh,
    keys,
    values,
    attended,
    gathered,
    member,
    totals_out,
    totals_core,
    totals_z,
    totals_y,
    decode_all,
    weights,
    cache_part,
    own_part,
    kept,
    core_out,
    core_in,
    z_out,
    z_in,
    y_out,
    y_in,
    wide_out,
    wide_in,
    own_sum,
    fresh_rows,
    part_out,
    part_in,
    load_sem,
    store_sem,
    ag_send,
    ag_recv,
    core_send,
    core_recv,
    z_send,
    z_recv,
    y_send,
    y_recv,
    row_send,
    row_recv,
    part_send,
    part_recv,
    tot_send,
    tot_recv,
    dec_send,
    dec_recv,
):
    g, t = lax.axis_index("grp"), lax.axis_index("tp")
    y, zh, core = g // (ZH * CORE), lax.rem(g // CORE, ZH), lax.rem(g, CORE)
    x, zl = t // ZL, lax.rem(t, ZL)

    def grp_of(y_at, zh_at, core_at):
        return (y_at * ZH + zh_at) * CORE + core_at

    def tp_of(x_off, flip):
        return lax.rem(x + x_off + X, X) * ZL + lax.rem(zl + flip, ZL)

    right, left, across = tp_of(1, 0), tp_of(-1, 0), tp_of(0, 1)

    def remote(src, dst, send, recv, device):
        return pltpu.make_async_remote_copy(
            src_ref=src,
            dst_ref=dst,
            send_sem=send,
            recv_sem=recv,
            device_id=device,
            device_id_type=MESH,
        )

    loads = [
        (cot_hbm, cot),
        (ids_hbm, ids),
        (rewards_hbm, rewards),
        (queries_hbm, queries),
        (fresh_hbm, fresh),
        (keys_hbm, keys),
        (decode_hbm.at[:, pl.ds(pl.multiple_of(t * WIDTH, 128), WIDTH)], decode_own),
        (learn_hbm, learn),
        (values_hbm, values),
        (master_hbm, adam_in.at[0]),
        (one_hbm, adam_in.at[1]),
        (two_hbm, adam_in.at[2]),
    ]
    loads = [pltpu.make_async_copy(src, dst, load_sem.at[i]) for i, (src, dst) in enumerate(loads)]
    for load in loads[:3]:
        load.start()
    (l_cot, l_ids, l_rewards, l_queries, l_fresh, l_keys, l_decode, l_learn, l_values, *l_adam) = loads

    barrier = pltpu.get_barrier_semaphore()

    def greet(device):
        pl.semaphore_signal(barrier, inc=1, device_id=device, device_id_type=MESH)

    for peer in (right, left, across):
        greet((g, peer))
    greet((grp_of(y, zh, 1 - core), t))
    for d in range(1, ZH):
        greet((grp_of(y, lax.rem(zh + d, ZH), core), t))
    for d in range(1, Y):
        greet((grp_of(lax.rem(y + d, Y), zh, core), t))
    l_cot.wait()
    turned = cot[...].T
    gathered[pl.ds(t * BLOCKS, BLOCKS)] = turned.reshape(BLOCKS, BLOCK, ROWS)

    pl.semaphore_wait(barrier, 3 + 1 + (ZH - 1) + (Y - 1))

    xl, xr, xx = tp_of(-1, 0), tp_of(1, 0), tp_of(2, 0)
    zo, zxl, zxr, zxx = tp_of(0, 1), tp_of(-1, 1), tp_of(1, 1), tp_of(2, 1)
    pieces = {
        "z0": (across, t, zo, 4, 4),
        "z1": (across, t, zo, 0, 4),
        "z2": (across, xl, zxl, 0, 1),
        "z3": (across, xr, zxr, 0, 1),
        "z4": (across, xx, zxx, 0, 4),
        "r0": (right, t, xl, 0, 4),
        "r1": (right, t, xl, 4, 4),
        "r2": (right, xl, xx, 0, 4),
        "r3": (right, zo, zxl, 4, 4),
        "r4": (right, zo, zxl, 1, 3),
        "r5": (right, zxl, zxx, 4, 2),
        "l0": (left, t, xr, 4, 4),
        "l1": (left, t, xr, 0, 4),
        "l2": (left, xr, xx, 4, 4),
        "l3": (left, zo, zxr, 4, 4),
        "l4": (left, zo, zxr, 1, 3),
        "l5": (left, zxr, zxx, 6, 2),
    }
    order = list(pieces)

    def piece(name, landed):
        peer, source, lands, first, count = pieces[name]
        blocks = gathered.at[pl.ds((lands if landed else source) * BLOCKS + first, count)]
        n = order.index(name)
        return remote(blocks, blocks, ag_send.at[n], ag_recv.at[n], (g, peer))

    def send(*names):
        for name in names:
            piece(name, False).start()

    def arrived(*names):
        for name in names:
            piece(name, True).wait_recv()

    send("z0", "r0", "l0")
    for load in loads[3:]:
        load.start()

    l_ids.wait()
    l_rewards.wait()
    group_at = lax.broadcasted_iota(jnp.int32, (GROUPS, ROWS), 0)
    id_row = jnp.concatenate([ids[k : k + 1, :] for k in range(ROWS // 128)], axis=1)
    reward_row = jnp.concatenate([rewards[k : k + 1, :] for k in range(ROWS // 128)], axis=1)
    member[...] = jnp.where(group_at == id_row, 1.0, 0.0).astype(bf16)
    high, middle, low = split_three(reward_row)
    rows = lax.broadcasted_iota(jnp.int32, (8, ROWS), 0)
    stack = jnp.where(
        rows == 0,
        high.astype(f32),
        jnp.where(rows == 1, middle.astype(f32), jnp.where(rows == 2, low.astype(f32), 1.0)),
    )
    totals_out[0] = dot(stack.astype(bf16), member[...], ((1,), (1,)))
    totals_of_core = remote(
        totals_out.at[0], totals_core, tot_send.at[0], tot_recv.at[0], (grp_of(y, zh, 1 - core), t)
    )
    totals_of_core.start()
    send("r1", "l1")

    totals_of_core.wait_recv()
    totals_out[1] = totals_out[0] + totals_core[...]

    def totals_over_z(d, landed):
        to, source = lax.rem(zh + d, ZH), lax.rem(zh - d + ZH, ZH)
        return remote(
            totals_out.at[1],
            totals_z.at[source if landed else zh],
            tot_send.at[d],
            tot_recv.at[d],
            (grp_of(y, to, core), t),
        )

    for d in FAR_Z:
        totals_over_z(d, False).start()
    send("z1")

    total = totals_out[1]
    for d in range(1, ZH):
        totals_over_z(d, True).wait_recv()
        total = total + totals_z[lax.rem(zh - d + ZH, ZH)]
    totals_out[2] = total

    def totals_over_y(d, landed):
        to, source = lax.rem(y + d, Y), lax.rem(y - d + Y, Y)
        return remote(
            totals_out.at[2],
            totals_y.at[source if landed else y],
            tot_send.at[ZH + d],
            tot_recv.at[ZH + d],
            (grp_of(to, zh, core), t),
        )

    for d in FAR_Y:
        totals_over_y(d, False).start()

    l_decode.wait()
    decode_all[core, y] = decode_own[...].astype(f32)

    def decode_copy(d, landed):
        to, source = lax.rem(y + d, Y), lax.rem(y - d + Y, Y)
        block = decode_all.at[core, source if landed else y]
        return remote(block, block, dec_send.at[d], dec_recv.at[d], (grp_of(to, zh, core), t))

    for d in range(1, Y):
        decode_copy(d, False).start()

    arrived("r0")
    send("r2", "z2")
    arrived("l0")
    send("l2")

    for d in range(1, Y):
        totals_over_y(d, True).wait_recv()
        total = total + totals_y[lax.rem(y - d + Y, Y)]

    size = total[3:4]
    mean = jnp.where(
        size > 0.5, (total[0:1] + total[1:2] + total[2:3]) / jnp.maximum(size, 1.0), 0.0
    )
    high, middle, low = split_three(mean)
    rows = lax.broadcasted_iota(jnp.int32, (8, GROUPS), 0)
    stack = jnp.where(
        rows == 0,
        high.astype(f32),
        jnp.where(rows == 1, middle.astype(f32), jnp.where(rows == 2, low.astype(f32), 0.0)),
    )
    means = dot(stack.astype(bf16), member[...], ((1,), (0,)))
    advantage = (reward_row - (means[0:1] + means[1:2] + means[2:3])) / float(ROWS)
    l_learn.wait()
    for k in range(ROWS // 128):
        column = jnp.broadcast_to(advantage[:, k * 128 : (k + 1) * 128], (128, 128)).T
        scaled = learn[k * 128 : (k + 1) * 128, :].astype(f32) * jnp.concatenate(
            [column] * (WIDTH // 128), axis=1
        )
        learn[k * 128 : (k + 1) * 128, :] = scaled.astype(bf16)

    def head_of(step):
        x_off = jnp.where(
            jnp.logical_or(step == 1, step == 5),
            X - 1,
            jnp.where(
                jnp.logical_or(step == 2, step == 6),
                1,
                jnp.where(jnp.logical_or(step == 4, step == 7), 2, 0),
            ),
        )
        flip = jnp.where(jnp.logical_or(step == 3, step >= 5), 1, 0)
        return tp_of(x_off, flip)

    def core_copy(step):
        return remote(
            core_out.at[step],
            core_in.at[step],
            core_send.at[step],
            core_recv.at[step],
            (grp_of(y, zh, 1 - core), t),
        )

    def z_copy(step, d, landed):
        to, source = lax.rem(zh + d, ZH), lax.rem(zh - d + ZH, ZH)
        return remote(
            z_out.at[step, to],
            z_in.at[step, source if landed else zh],
            z_send.at[step * ZH + d],
            z_recv.at[step * ZH + d],
            (grp_of(y, to, core), t),
        )

    def y_copy(step, head):
        return remote(
            y_out.at[step], y_in.at[y], y_send.at[step], y_recv.at[y], (grp_of(head, zh, core), t)
        )

    def wide_copy(step, head):
        return remote(
            wide_out.at[step], wide_in.at[y], y_send.at[step], y_recv.at[y], (grp_of(head, zh, core), t)
        )

    star = jnp.where(y == head_of(0), 0, jnp.where(y == head_of(1), 1, 2))
    early = jnp.logical_or(star < 2, y == head_of(2))

    def over_z(step, block):
        kept[step] = block
        z_out[step] = block.astype(bf16).reshape(ZH, BLOCK, WIDTH)
        for d in FAR_Z:
            z_copy(step, d, False).start()

    def z_total(step):
        total = kept[step, pl.ds(pl.multiple_of(zh * BLOCK, BLOCK), BLOCK)]
        for d in range(1, ZH):
            z_copy(step, d, True).wait_recv()
            total = total + z_in[step, lax.rem(zh - d + ZH, ZH)].astype(f32)
        return total

    def from_core(step):
        core_copy(step).wait_recv()
        over_z(step, kept[step] + core_in[step].astype(f32))

    def from_core_wide(step):
        core_copy(step).wait_recv()
        both = kept[step] + core_in[step].astype(f32)
        kept[step] = both
        head = head_of(step)

        @pl.when(head != y)
        def _():
            wide_out[step] = both.astype(bf16)
            wide_copy(step, head).start()

    def from_z(step, _):
        total = z_total(step)
        head = head_of(step)

        @pl.when(head == y)
        def _():
            own_sum[...] = total

        @pl.when(head != y)
        def _():
            y_out[step] = total.astype(bf16)
            y_copy(step, head).start()

        return 0

    def rows_of(step, parity):
        base = head_of(step) * BLOCKS
        return [gathered[base + 2 * k + parity] for k in range(ZH)]

    last = TP - 1
    quarter = HALF // 2

    def last_copy(half):
        rows = pl.ds(half * quarter, quarter)
        return remote(
            core_out.at[last, rows],
            core_in.at[last, rows],
            core_send.at[last + half],
            core_recv.at[last + half],
            (grp_of(y, zh, 1 - core), t),
        )

    def multiply_last(half):
        chosen = slice(half * (ZH // 2), (half + 1) * (ZH // 2))
        lhs = rows_of(last, 1 - core)[chosen] + rows_of(last, core)[chosen]
        result = dot(jnp.concatenate(lhs, axis=0), learn[...], ((1,), (0,)))
        rows = slice(half * quarter, (half + 1) * quarter)
        core_out[last, rows] = result[:quarter].astype(bf16)
        last_copy(half).start()
        kept[last, rows] = result[quarter:]

    def from_core_last(half):
        last_copy(half).wait_recv()
        rows = slice(half * quarter, (half + 1) * quarter)
        both = kept[last, rows] + core_in[last, rows].astype(f32)
        kept[last, rows] = both
        blocks = slice(half * (ZH // 2), (half + 1) * (ZH // 2))
        z_out[last, blocks] = both.astype(bf16).reshape(ZH // 2, BLOCK, WIDTH)
        for d in FAR_Z:
            to = lax.rem(zh + d, ZH)

            @pl.when((to >= ZH // 2) if half else (to < ZH // 2))
            def _():
                z_copy(last, d, False).start()

    def multiply(heads):
        lhs = [rows_of(head, 1 - core) + rows_of(head, core) for head in heads]
        result = dot(jnp.concatenate(sum(lhs, []), axis=0), learn[...], ((1,), (0,)))
        for n, head in enumerate(heads):
            core_out[head] = result[2 * n * HALF : (2 * n + 1) * HALF].astype(bf16)
            core_copy(head).start()
            kept[head] = result[(2 * n + 1) * HALF : (2 * n + 2) * HALF]

    def one_step(step, _):
        @pl.when(step == 0)
        def _():
            arrived("r1")

        @pl.when(step == 1)
        def _():
            arrived("z0")
            send("r3", "l3")
            arrived("l1")
            send("z3")
            arrived("z1")
            send("r4", "l4")

        @pl.when(step == 2)
        def _():
            arrived("r2", "l2")
            send("z4")

        @pl.when(step == 3)
        def _():
            arrived("r3", "l3")
            send("r5", "l5")
            arrived("r4", "z2", "l4", "z3")

        first = 2 * step - jnp.where(step >= 3, 1, 0)

        @pl.when(step == 2)
        def _():
            multiply([first])

        @pl.when(step != 2)
        def _():
            multiply([first, first + 1])

        @pl.when(step == 1)
        def _():
            from_core_wide(0)
            from_core_wide(1)

        @pl.when(step == 2)
        def _():
            from_core_wide(2)
            from_core(3)

        @pl.when(step == 3)
        def _():
            from_core(4)
            from_z(3, 0)

        return 0

    lax.fori_loop(0, 4, one_step, 0)
    arrived("z4")
    multiply_last(0)
    from_core(5)
    from_core(6)
    from_z(4, 0)
    from_core_last(0)
    arrived("r5", "l5")
    multiply_last(1)

    def decode_across(at):
        block = decode_all.at[at]
        return remote(block, block, dec_send.at[0], dec_recv.at[0], (grp_of(y, zh, 1 - core), t))

    for d in range(1, Y):
        decode_copy(d, True).wait_recv()
    decode_across(core).start()
    from_core_last(1)

    lax.fori_loop(5, TP - 1, from_z, 0)

    @pl.when(early)
    def _():
        block = kept[star]
        for d in range(1, Y):
            source = lax.rem(y - d + Y, Y)
            landed = wide_in.at[source]
            remote(landed, landed, y_send.at[0], y_recv.at[source], (g, right)).wait_recv()
            block = block + wide_in[source].astype(f32)
        over_z(star, block)

    l_queries.wait()
    l_fresh.wait()
    l_keys.wait()
    scale = 1.0 / math.sqrt(HEAD_SIZE)
    tiles = queries[...].astype(f32)
    tiles = jnp.concatenate(
        [tiles[:, j * HEAD_SIZE : (j + 1) * HEAD_SIZE] for j in range(QUERIES)], axis=0
    )
    query_rows = tiles.astype(bf16)
    row_of = lax.broadcasted_iota(jnp.int32, (QUERIES * DECODE, SLOTS), 0) & (DECODE - 1)
    slot_of = lax.broadcasted_iota(jnp.int32, (QUERIES * DECODE, SLOTS), 1)
    scores = jnp.zeros((QUERIES * DECODE, SLOTS), f32)
    for r in range(DECODE):
        of_row = dot(query_rows, keys[r], ((1,), (1,))) * scale
        of_row = jnp.where(slot_of < lengths_ref[r], of_row, -jnp.inf)
        scores = jnp.where(row_of == r, of_row, scores)
    fresh_tiles = jnp.concatenate([fresh[...].astype(f32)] * QUERIES, axis=0)
    own_score = jnp.sum(tiles * fresh_tiles, axis=1, keepdims=True) * scale
    highest = jnp.maximum(jnp.max(scores, axis=1, keepdims=True), own_score)
    cache_exp = jnp.exp(scores - highest)
    own_exp = jnp.exp(own_score - highest)
    denominator = jnp.sum(cache_exp, axis=1, keepdims=True) + own_exp
    weights[...] = (cache_exp / denominator).astype(bf16)
    own_weight = (own_exp / denominator).astype(bf16).astype(f32)
    own_part[...] = jnp.broadcast_to(own_weight, (QUERIES * DECODE, HEAD_SIZE))

    from_z(TP - 1, 0)

    l_values.wait()
    row_at = lax.broadcasted_iota(jnp.int32, (QUERIES * DECODE, HEAD_SIZE), 0) & (DECODE - 1)
    cached = jnp.zeros((QUERIES * DECODE, HEAD_SIZE), f32)
    for r in range(DECODE):
        of_row = dot(weights[...], values[r], ((1,), (0,)))
        cached = jnp.where(row_at == r, of_row, cached)
    cache_part[...] = cached

    for owner in range(ZH):
        fresh_rows[owner * CORE + 1 - core] = jnp.zeros((BLOCK, WIDTH), bf16)

    @pl.when(early)
    def _():
        own_sum[...] = z_total(star)

    @pl.when(jnp.logical_not(early))
    def _():
        total = own_sum[...]
        for d in range(1, Y):
            source = lax.rem(y - d + Y, Y)
            landed = y_in.at[source]
            remote(landed, landed, y_send.at[0], y_recv.at[source], (g, right)).wait_recv()
            total = total + y_in[source].astype(f32)
        own_sum[...] = total

    for load in l_adam:
        load.wait()
    gradient = own_sum[...]

    updated, _, _ = optimizer_step(gradient, adam_in[0], adam_in[1], adam_in[2])

    mine = zh * CORE + core

    def row_copy(d, landed):
        to, source = lax.rem(zh + d, ZH), lax.rem(zh - d + ZH, ZH)
        block = fresh_rows.at[(source if landed else zh) * CORE + core]
        return remote(block, block, row_send.at[d], row_recv.at[d], (grp_of(y, to, core), t))

    fresh_rows[mine] = updated.astype(bf16)
    for d in FAR_Z:
        row_copy(d, False).start()
    store = pltpu.make_async_copy(own_sum, gradient_hbm, store_sem.at[0])
    store.start()
    decode_across(1 - core).wait_recv()
    decode = decode_all[...].reshape(CORE * Y * DECODE, WIDTH).astype(bf16)

    for name in order:
        piece(name, False).wait_send()
    totals_of_core.wait_send()
    for d in range(1, ZH):
        totals_over_z(d, False).wait_send()
    for d in range(1, Y):
        totals_over_y(d, False).wait_send()
        decode_copy(d, False).wait_send()
    decode_across(core).wait_send()
    for step in range(TP):
        if step == last:
            last_copy(0).wait_send()
            last_copy(1).wait_send()
        else:
            core_copy(step).wait_send()
        head = head_of(step)
        if step >= WIDE:
            for d in range(1, ZH):
                z_copy(step, d, False).wait_send()

        @pl.when(head != y)
        def _():
            (y_copy if step >= WIDE else wide_copy)(step, head).wait_send()

    @pl.when(early)
    def _():
        for d in range(1, ZH):
            z_copy(star, d, False).wait_send()

    for d in range(1, ZH):
        row_copy(d, True).wait_recv()

    part = dot(decode, fresh_rows[...].reshape(HEAD_SIZE, WIDTH), ((1,), (1,)))
    part_out[...] = part.reshape(CORE, Y, DECODE, HEAD_SIZE)

    def part_copy(of_core, d):
        to = lax.rem(y + d, Y)
        return remote(
            part_out.at[of_core, to],
            part_in.at[core, t],
            part_send.at[of_core * Y + to],
            part_recv.at[core * TP + t],
            (grp_of(to, zh, of_core), y),
        )

    for d in FAR_Y:
        part_copy(core, d).start()
        part_copy(1 - core, d).start()
    part_copy(1 - core, 0).start()

    @pl.when(t == y)
    def _():
        part_in[core, t] = part_out[core, y]

    @pl.when(t != y)
    def _():
        part_copy(core, 0).start()

    def part_arrived(of_core, d):
        source = lax.rem(t + d, TP)
        landed = part_in.at[of_core, source]
        remote(
            landed,
            landed,
            part_send.at[0],
            part_recv.at[of_core * TP + source],
            (grp_of(y, zh, 1 - core), t),
        ).wait_recv()

    for d in range(1, TP):
        part_arrived(core, d)
        part_arrived(1 - core, d)
    part_arrived(1 - core, 0)

    @pl.when(t != y)
    def _():
        part_arrived(core, 0)

    new_values = jnp.sum(part_in[...].reshape(CORE * TP, DECODE, HEAD_SIZE), axis=0)
    new_values = new_values.astype(bf16).astype(f32)
    outcome = cache_part[...] + own_part[...] * jnp.concatenate([new_values] * QUERIES, axis=0)
    attended[...] = jnp.concatenate(
        [outcome[j * DECODE : (j + 1) * DECODE] for j in range(QUERIES)], axis=1
    )
    result_store = pltpu.make_async_copy(attended, attended_hbm, store_sem.at[1])
    result_store.start()

    for d in range(1, ZH):
        row_copy(d, False).wait_send()
    for d in range(Y):
        part_copy(1 - core, d).wait_send()
    for d in range(1, Y):
        part_copy(core, d).wait_send()

    @pl.when(t != y)
    def _():
        part_copy(core, 0).wait_send()

    store.wait()
    result_store.wait()


def finish_kernel(gradient, master, one, two, attended, new_master, new_one, new_two, rounded):
    new_master[...], new_one[...], new_two[...] = optimizer_step(
        gradient[...], master[...], one[...], two[...]
    )
    rounded[...] = attended[...].astype(bf16)


def per_device(
    learn_rows,
    cot_values,
    rewards,
    group_ids,
    master,
    moment_one,
    moment_two,
    decode_rows,
    queries,
    fresh_keys,
    stored_keys,
    stored_values,
    cache_lengths,
):
    dma = pltpu.SemaphoreType.DMA
    shard = jax.ShapeDtypeStruct((BLOCK, WIDTH), f32)
    heads = QUERIES * HEAD_SIZE
    scratch = [
        ((ROWS, HEAD_SIZE), bf16),
        ((ROWS, WIDTH), bf16),
        ((ROWS // 128, 128), f32),
        ((ROWS // 128, 128), jnp.int32),
        ((3, BLOCK, WIDTH), f32),
        ((DECODE, WIDTH), bf16),
        ((DECODE, heads), bf16),
        ((DECODE, HEAD_SIZE), bf16),
        ((DECODE, SLOTS, HEAD_SIZE), bf16),
        ((DECODE, SLOTS, HEAD_SIZE), bf16),
        ((DECODE, heads), f32),
        ((TP * BLOCKS, BLOCK, ROWS), bf16),
        ((GROUPS, ROWS), bf16),
        ((3, 8, GROUPS), f32),
        ((8, GROUPS), f32),
        ((ZH, 8, GROUPS), f32),
        ((Y, 8, GROUPS), f32),
        ((CORE, Y, DECODE, WIDTH), f32),
        ((QUERIES * DECODE, SLOTS), bf16),
        ((QUERIES * DECODE, HEAD_SIZE), f32),
        ((QUERIES * DECODE, HEAD_SIZE), f32),
        ((TP, HALF, WIDTH), f32),
        ((TP, HALF, WIDTH), bf16),
        ((TP, HALF, WIDTH), bf16),
        ((TP, ZH, BLOCK, WIDTH), bf16),
        ((TP, ZH, BLOCK, WIDTH), bf16),
        ((TP, BLOCK, WIDTH), bf16),
        ((Y, BLOCK, WIDTH), bf16),
        ((WIDE, HALF, WIDTH), bf16),
        ((Y, HALF, WIDTH), bf16),
        ((BLOCK, WIDTH), f32),
        ((ZH * CORE, BLOCK, WIDTH), bf16),
        ((CORE, Y, DECODE, HEAD_SIZE), f32),
        ((CORE, TP, DECODE, HEAD_SIZE), f32),
    ]
    semaphores = [12, 2, 17, 17, TP + 1, TP + 1, TP * ZH, TP * ZH, TP, Y, ZH, ZH, CORE * Y, CORE * TP, ZH + Y, ZH + Y, Y, Y]
    hbm = pl.BlockSpec(memory_space=pltpu.HBM)
    gradient, attended = pl.pallas_call(
        kernel,
        out_shape=(shard, jax.ShapeDtypeStruct((DECODE, heads), f32)),
        in_specs=[hbm] * 12 + [pl.BlockSpec(memory_space=pltpu.SMEM)],
        out_specs=[hbm] * 2,
        scratch_shapes=[pltpu.VMEM(shape, kind) for shape, kind in scratch]
        + [dma((n,)) for n in semaphores],
        compiler_params=pltpu.CompilerParams(
            collective_id=0, has_side_effects=True, vmem_limit_bytes=60 * 1024 * 1024
        ),
    )(
        cot_values,
        learn_rows,
        rewards.reshape(ROWS // 128, 128),
        group_ids.reshape(ROWS // 128, 128),
        master,
        moment_one,
        moment_two,
        decode_rows,
        queries,
        fresh_keys,
        stored_keys,
        stored_values,
        cache_lengths,
    )
    return pl.pallas_call(
        finish_kernel,
        out_shape=(shard, shard, shard, jax.ShapeDtypeStruct((DECODE, heads), bf16)),
    )(gradient, master, moment_one, moment_two, attended)


def solution(mesh):
    shards, rows = P("grp", "tp"), P("grp")
    cache = P("grp", None, "tp")
    in_specs = (
        shards,
        shards,
        rows,
        rows,
        shards,
        shards,
        shards,
        P("grp", None),
        shards,
        shards,
        cache,
        cache,
        rows,
    )
    return jax.shard_map(
        per_device, mesh=mesh, in_specs=in_specs, out_specs=(shards,) * 4, check_vma=False
    )
```

```python
import math

import jax
import jax.numpy as jnp
from jax import lax
from jax.experimental import pallas as pl
from jax.experimental.pallas import tpu as pltpu
from jax.sharding import PartitionSpec as P

HEAD_SIZE = 128
QUERIES = 8
ROWS = 1536
WIDTH = 640
GROUPS = 256
SLOTS = 256
DECODE = 8
Y, ZH, CORE, X, ZL = 8, 4, 2, 4, 2
TP = X * ZL
BLOCKS = 8
BLOCK = 16
HALF = 64
WIDE = 3
FAR_Z = (2, 1, 3)
FAR_Y = (4, 3, 5, 2, 6, 1, 7)

beta_one = 0.9
beta_two = 0.95
learning_rate = 0.001
weight_decay = 0.1
adam_epsilon = 1e-08
step_count = 2.0

MESH = pl.DeviceIdType.MESH
bf16, f32 = jnp.bfloat16, jnp.float32


def split_three(value):
    high = value.astype(bf16)
    rest = value - high.astype(f32)
    middle = rest.astype(bf16)
    low = (rest - middle.astype(f32)).astype(bf16)
    return high, middle, low


def optimizer_step(gradient, master, moment_one, moment_two):
    first = beta_one * moment_one + (1.0 - beta_one) * gradient
    second = beta_two * moment_two + (1.0 - beta_two) * gradient * gradient
    first_hat = first / (1.0 - beta_one**step_count)
    second_hat = second / (1.0 - beta_two**step_count)
    updated = master - learning_rate * (
        first_hat / (jnp.sqrt(second_hat) + adam_epsilon) + weight_decay * master
    )
    return updated, first, second


def dot(a, b, dims):
    return lax.dot_general(a, b, (dims, ((), ())), preferred_element_type=f32)


def kernel(
    cot_hbm,
    learn_hbm,
    rewards_hbm,
    ids_hbm,
    master_hbm,
    one_hbm,
    two_hbm,
    decode_hbm,
    queries_hbm,
    fresh_hbm,
    keys_hbm,
    values_hbm,
    lengths_ref,
    gradient_hbm,
    attended_hbm,
    cot,
    learn,
    rewards,
    ids,
    adam_in,
    decode_own,
    queries,
    fresh,
    keys,
    values,
    attended,
    gathered,
    member,
    totals_out,
    totals_core,
    totals_z,
    totals_y,
    decode_all,
    weights,
    cache_part,
    own_part,
    kept,
    core_out,
    core_in,
    z_out,
    z_in,
    y_out,
    y_in,
    wide_out,
    wide_in,
    own_sum,
    fresh_rows,
    part_out,
    part_in,
    load_sem,
    store_sem,
    ag_send,
    ag_recv,
    core_send,
    core_recv,
    z_send,
    z_recv,
    y_send,
    y_recv,
    row_send,
    row_recv,
    part_send,
    part_recv,
    tot_send,
    tot_recv,
    dec_send,
    dec_recv,
):
    g, t = lax.axis_index("grp"), lax.axis_index("tp")
    y, zh, core = g // (ZH * CORE), lax.rem(g // CORE, ZH), lax.rem(g, CORE)
    x, zl = t // ZL, lax.rem(t, ZL)

    def grp_of(y_at, zh_at, core_at):
        return (y_at * ZH + zh_at) * CORE + core_at

    def tp_of(x_off, flip):
        return lax.rem(x + x_off + X, X) * ZL + lax.rem(zl + flip, ZL)

    right, left, across = tp_of(1, 0), tp_of(-1, 0), tp_of(0, 1)

    def remote(src, dst, send, recv, device):
        return pltpu.make_async_remote_copy(
            src_ref=src,
            dst_ref=dst,
            send_sem=send,
            recv_sem=recv,
            device_id=device,
            device_id_type=MESH,
        )

    loads = [
        (cot_hbm, cot),
        (ids_hbm, ids),
        (rewards_hbm, rewards),
        (queries_hbm, queries),
        (fresh_hbm, fresh),
        (keys_hbm, keys),
        (decode_hbm.at[:, pl.ds(pl.multiple_of(t * WIDTH, 128), WIDTH)], decode_own),
        (learn_hbm, learn),
        (values_hbm, values),
        (master_hbm, adam_in.at[0]),
        (one_hbm, adam_in.at[1]),
        (two_hbm, adam_in.at[2]),
    ]
    loads = [pltpu.make_async_copy(src, dst, load_sem.at[i]) for i, (src, dst) in enumerate(loads)]
    for load in loads[:3]:
        load.start()
    (l_cot, l_ids, l_rewards, l_queries, l_fresh, l_keys, l_decode, l_learn, l_values, *l_adam) = loads

    barrier = pltpu.get_barrier_semaphore()

    def greet(device):
        pl.semaphore_signal(barrier, inc=1, device_id=device, device_id_type=MESH)

    for peer in (right, left, across):
        greet((g, peer))
    greet((grp_of(y, zh, 1 - core), t))
    for d in range(1, ZH):
        greet((grp_of(y, lax.rem(zh + d, ZH), core), t))
    for d in range(1, Y):
        greet((grp_of(lax.rem(y + d, Y), zh, core), t))
    l_cot.wait()
    turned = cot[...].T
    gathered[pl.ds(t * BLOCKS, BLOCKS)] = turned.reshape(BLOCKS, BLOCK, ROWS)

    pl.semaphore_wait(barrier, 3 + 1 + (ZH - 1) + (Y - 1))

    xl, xr, xx = tp_of(-1, 0), tp_of(1, 0), tp_of(2, 0)
    zo, zxl, zxr, zxx = tp_of(0, 1), tp_of(-1, 1), tp_of(1, 1), tp_of(2, 1)
    pieces = {
        "z0": (across, t, zo, 4, 4),
        "z1": (across, t, zo, 0, 4),
        "z2": (across, xl, zxl, 0, 1),
        "z3": (across, xr, zxr, 0, 1),
        "z4": (across, xx, zxx, 0, 4),
        "r0": (right, t, xl, 0, 4),
        "r1": (right, t, xl, 4, 4),
        "r2": (right, xl, xx, 0, 4),
        "r3": (right, zo, zxl, 4, 4),
        "r4": (right, zo, zxl, 1, 3),
        "r5": (right, zxl, zxx, 4, 2),
        "l0": (left, t, xr, 4, 4),
        "l1": (left, t, xr, 0, 4),
        "l2": (left, xr, xx, 4, 4),
        "l3": (left, zo, zxr, 4, 4),
        "l4": (left, zo, zxr, 1, 3),
        "l5": (left, zxr, zxx, 6, 2),
    }
    order = list(pieces)

    def piece(name, landed):
        peer, source, lands, first, count = pieces[name]
        blocks = gathered.at[pl.ds((lands if landed else source) * BLOCKS + first, count)]
        n = order.index(name)
        return remote(blocks, blocks, ag_send.at[n], ag_recv.at[n], (g, peer))

    def send(*names):
        for name in names:
            piece(name, False).start()

    def arrived(*names):
        for name in names:
            piece(name, True).wait_recv()

    send("z0", "r0", "l0")
    for load in loads[3:]:
        load.start()

    l_ids.wait()
    l_rewards.wait()
    group_at = lax.broadcasted_iota(jnp.int32, (GROUPS, ROWS), 0)
    id_row = jnp.concatenate([ids[k : k + 1, :] for k in range(ROWS // 128)], axis=1)
    reward_row = jnp.concatenate([rewards[k : k + 1, :] for k in range(ROWS // 128)], axis=1)
    member[...] = jnp.where(group_at == id_row, 1.0, 0.0).astype(bf16)
    high, middle, low = split_three(reward_row)
    rows = lax.broadcasted_iota(jnp.int32, (8, ROWS), 0)
    stack = jnp.where(
        rows == 0,
        high.astype(f32),
        jnp.where(rows == 1, middle.astype(f32), jnp.where(rows == 2, low.astype(f32), 1.0)),
    )
    totals_out[0] = dot(stack.astype(bf16), member[...], ((1,), (1,)))
    totals_of_core = remote(
        totals_out.at[0], totals_core, tot_send.at[0], tot_recv.at[0], (grp_of(y, zh, 1 - core), t)
    )
    totals_of_core.start()
    send("r1", "l1")

    totals_of_core.wait_recv()
    totals_out[1] = totals_out[0] + totals_core[...]

    def totals_over_z(d, landed):
        to, source = lax.rem(zh + d, ZH), lax.rem(zh - d + ZH, ZH)
        return remote(
            totals_out.at[1],
            totals_z.at[source if landed else zh],
            tot_send.at[d],
            tot_recv.at[d],
            (grp_of(y, to, core), t),
        )

    for d in FAR_Z:
        totals_over_z(d, False).start()
    send("z1")

    total = totals_out[1]
    for d in range(1, ZH):
        totals_over_z(d, True).wait_recv()
        total = total + totals_z[lax.rem(zh - d + ZH, ZH)]
    totals_out[2] = total

    def totals_over_y(d, landed):
        to, source = lax.rem(y + d, Y), lax.rem(y - d + Y, Y)
        return remote(
            totals_out.at[2],
            totals_y.at[source if landed else y],
            tot_send.at[ZH + d],
            tot_recv.at[ZH + d],
            (grp_of(to, zh, core), t),
        )

    for d in FAR_Y:
        totals_over_y(d, False).start()

    l_decode.wait()
    decode_all[core, y] = decode_own[...].astype(f32)

    def decode_copy(d, landed):
        to, source = lax.rem(y + d, Y), lax.rem(y - d + Y, Y)
        block = decode_all.at[core, source if landed else y]
        return remote(block, block, dec_send.at[d], dec_recv.at[d], (grp_of(to, zh, core), t))

    for d in range(1, Y):
        decode_copy(d, False).start()

    arrived("r0")
    send("r2", "z2")
    arrived("l0")
    send("l2")

    l_queries.wait()
    l_fresh.wait()
    l_keys.wait()
    scale = 1.0 / math.sqrt(HEAD_SIZE)
    tiles = queries[...].astype(f32)
    tiles = jnp.concatenate(
        [tiles[:, j * HEAD_SIZE : (j + 1) * HEAD_SIZE] for j in range(QUERIES)], axis=0
    )
    query_rows = tiles.astype(bf16)
    row_of = lax.broadcasted_iota(jnp.int32, (QUERIES * DECODE, SLOTS), 0) & (DECODE - 1)
    slot_of = lax.broadcasted_iota(jnp.int32, (QUERIES * DECODE, SLOTS), 1)
    scores = jnp.zeros((QUERIES * DECODE, SLOTS), f32)
    for r in range(DECODE):
        of_row = dot(query_rows, keys[r], ((1,), (1,))) * scale
        of_row = jnp.where(slot_of < lengths_ref[r], of_row, -jnp.inf)
        scores = jnp.where(row_of == r, of_row, scores)
    fresh_tiles = jnp.concatenate([fresh[...].astype(f32)] * QUERIES, axis=0)
    own_score = jnp.sum(tiles * fresh_tiles, axis=1, keepdims=True) * scale
    highest = jnp.maximum(jnp.max(scores, axis=1, keepdims=True), own_score)
    cache_exp = jnp.exp(scores - highest)
    own_exp = jnp.exp(own_score - highest)
    denominator = jnp.sum(cache_exp, axis=1, keepdims=True) + own_exp
    weights[...] = (cache_exp / denominator).astype(bf16)
    own_weight = (own_exp / denominator).astype(bf16).astype(f32)
    own_part[...] = jnp.broadcast_to(own_weight, (QUERIES * DECODE, HEAD_SIZE))

    l_values.wait()
    row_at = lax.broadcasted_iota(jnp.int32, (QUERIES * DECODE, HEAD_SIZE), 0) & (DECODE - 1)
    cached = jnp.zeros((QUERIES * DECODE, HEAD_SIZE), f32)
    for r in range(DECODE):
        of_row = dot(weights[...], values[r], ((1,), (0,)))
        cached = jnp.where(row_at == r, of_row, cached)
    cache_part[...] = cached

    for owner in range(ZH):
        fresh_rows[owner * CORE + 1 - core] = jnp.zeros((BLOCK, WIDTH), bf16)

    for d in range(1, Y):
        totals_over_y(d, True).wait_recv()
        total = total + totals_y[lax.rem(y - d + Y, Y)]

    size = total[3:4]
    mean = jnp.where(
        size > 0.5, (total[0:1] + total[1:2] + total[2:3]) / jnp.maximum(size, 1.0), 0.0
    )
    high, middle, low = split_three(mean)
    rows = lax.broadcasted_iota(jnp.int32, (8, GROUPS), 0)
    stack = jnp.where(
        rows == 0,
        high.astype(f32),
        jnp.where(rows == 1, middle.astype(f32), jnp.where(rows == 2, low.astype(f32), 0.0)),
    )
    means = dot(stack.astype(bf16), member[...], ((1,), (0,)))
    advantage = (reward_row - (means[0:1] + means[1:2] + means[2:3])) / float(ROWS)
    l_learn.wait()
    for k in range(ROWS // 128):
        column = jnp.broadcast_to(advantage[:, k * 128 : (k + 1) * 128], (128, 128)).T
        scaled = learn[k * 128 : (k + 1) * 128, :].astype(f32) * jnp.concatenate(
            [column] * (WIDTH // 128), axis=1
        )
        learn[k * 128 : (k + 1) * 128, :] = scaled.astype(bf16)

    def head_of(step):
        x_off = jnp.where(
            jnp.logical_or(step == 1, step == 5),
            X - 1,
            jnp.where(
                jnp.logical_or(step == 2, step == 6),
                1,
                jnp.where(jnp.logical_or(step == 4, step == 7), 2, 0),
            ),
        )
        flip = jnp.where(jnp.logical_or(step == 3, step >= 5), 1, 0)
        return tp_of(x_off, flip)

    def core_copy(step):
        return remote(
            core_out.at[step],
            core_in.at[step],
            core_send.at[step],
            core_recv.at[step],
            (grp_of(y, zh, 1 - core), t),
        )

    def z_copy(step, d, landed):
        to, source = lax.rem(zh + d, ZH), lax.rem(zh - d + ZH, ZH)
        return remote(
            z_out.at[step, to],
            z_in.at[step, source if landed else zh],
            z_send.at[step * ZH + d],
            z_recv.at[step * ZH + d],
            (grp_of(y, to, core), t),
        )

    def y_copy(step, head):
        return remote(
            y_out.at[step], y_in.at[y], y_send.at[step], y_recv.at[y], (grp_of(head, zh, core), t)
        )

    def wide_copy(step, head):
        return remote(
            wide_out.at[step], wide_in.at[y], y_send.at[step], y_recv.at[y], (grp_of(head, zh, core), t)
        )

    star = jnp.where(y == head_of(0), 0, jnp.where(y == head_of(1), 1, 2))
    early = jnp.logical_or(star < 2, y == head_of(2))

    def over_z(step, block):
        kept[step] = block
        z_out[step] = block.astype(bf16).reshape(ZH, BLOCK, WIDTH)
        for d in FAR_Z:
            z_copy(step, d, False).start()

    def z_total(step):
        total = kept[step, pl.ds(pl.multiple_of(zh * BLOCK, BLOCK), BLOCK)]
        for d in range(1, ZH):
            z_copy(step, d, True).wait_recv()
            total = total + z_in[step, lax.rem(zh - d + ZH, ZH)].astype(f32)
        return total

    def from_core(step):
        core_copy(step).wait_recv()
        over_z(step, kept[step] + core_in[step].astype(f32))

    def from_core_wide(step):
        core_copy(step).wait_recv()
        both = kept[step] + core_in[step].astype(f32)
        kept[step] = both
        head = head_of(step)

        @pl.when(head != y)
        def _():
            wide_out[step] = both.astype(bf16)
            wide_copy(step, head).start()

    def from_z(step, _):
        total = z_total(step)
        head = head_of(step)

        @pl.when(head == y)
        def _():
            own_sum[...] = total

        @pl.when(head != y)
        def _():
            y_out[step] = total.astype(bf16)
            y_copy(step, head).start()

        return 0

    def rows_of(step, parity):
        base = head_of(step) * BLOCKS
        return [gathered[base + 2 * k + parity] for k in range(ZH)]

    last = TP - 1
    quarter = HALF // 2

    def last_copy(half):
        rows = pl.ds(half * quarter, quarter)
        return remote(
            core_out.at[last, rows],
            core_in.at[last, rows],
            core_send.at[last + half],
            core_recv.at[last + half],
            (grp_of(y, zh, 1 - core), t),
        )

    def multiply_last(half):
        chosen = slice(half * (ZH // 2), (half + 1) * (ZH // 2))
        lhs = rows_of(last, 1 - core)[chosen] + rows_of(last, core)[chosen]
        result = dot(jnp.concatenate(lhs, axis=0), learn[...], ((1,), (0,)))
        rows = slice(half * quarter, (half + 1) * quarter)
        core_out[last, rows] = result[:quarter].astype(bf16)
        last_copy(half).start()
        kept[last, rows] = result[quarter:]

    def from_core_last(half):
        last_copy(half).wait_recv()
        rows = slice(half * quarter, (half + 1) * quarter)
        both = kept[last, rows] + core_in[last, rows].astype(f32)
        kept[last, rows] = both
        blocks = slice(half * (ZH // 2), (half + 1) * (ZH // 2))
        z_out[last, blocks] = both.astype(bf16).reshape(ZH // 2, BLOCK, WIDTH)
        for d in FAR_Z:
            to = lax.rem(zh + d, ZH)

            @pl.when((to >= ZH // 2) if half else (to < ZH // 2))
            def _():
                z_copy(last, d, False).start()

    def multiply(heads):
        lhs = [rows_of(head, 1 - core) + rows_of(head, core) for head in heads]
        result = dot(jnp.concatenate(sum(lhs, []), axis=0), learn[...], ((1,), (0,)))
        for n, head in enumerate(heads):
            core_out[head] = result[2 * n * HALF : (2 * n + 1) * HALF].astype(bf16)
            core_copy(head).start()
            kept[head] = result[(2 * n + 1) * HALF : (2 * n + 2) * HALF]

    def decode_across(at):
        block = decode_all.at[at]
        return remote(block, block, dec_send.at[0], dec_recv.at[0], (grp_of(y, zh, 1 - core), t))

    def one_step(step, _):
        @pl.when(step == 0)
        def _():
            arrived("r1")

        @pl.when(step == 1)
        def _():
            arrived("z0")
            send("r3", "l3")
            arrived("l1")
            send("z3")
            arrived("z1")
            send("r4", "l4")

        @pl.when(step == 2)
        def _():
            arrived("r2", "l2")
            send("z4")

        @pl.when(step == 3)
        def _():
            arrived("r3", "l3")
            send("r5", "l5")
            for d in range(1, Y):
                decode_copy(d, True).wait_recv()
            decode_across(core).start()
            arrived("r4", "z2", "l4", "z3")

        first = 2 * step - jnp.where(step >= 3, 1, 0)

        @pl.when(step == 2)
        def _():
            multiply([first])

        @pl.when(step != 2)
        def _():
            multiply([first, first + 1])

        @pl.when(step == 1)
        def _():
            from_core_wide(0)
            from_core_wide(1)

        @pl.when(step == 2)
        def _():
            from_core_wide(2)
            from_core(3)

        @pl.when(step == 3)
        def _():
            from_core(4)
            from_z(3, 0)

        return 0

    lax.fori_loop(0, 4, one_step, 0)
    arrived("z4")
    multiply_last(0)
    from_core(5)
    from_core(6)
    from_z(4, 0)
    from_core_last(0)
    arrived("r5", "l5")
    multiply_last(1)

    from_core_last(1)

    lax.fori_loop(5, TP - 1, from_z, 0)

    @pl.when(early)
    def _():
        block = kept[star]
        for d in range(1, Y):
            source = lax.rem(y - d + Y, Y)
            landed = wide_in.at[source]
            remote(landed, landed, y_send.at[0], y_recv.at[source], (g, right)).wait_recv()
            block = block + wide_in[source].astype(f32)
        over_z(star, block)

    from_z(TP - 1, 0)

    @pl.when(early)
    def _():
        own_sum[...] = z_total(star)

    @pl.when(jnp.logical_not(early))
    def _():
        total = own_sum[...]
        for d in range(1, Y):
            source = lax.rem(y - d + Y, Y)
            landed = y_in.at[source]
            remote(landed, landed, y_send.at[0], y_recv.at[source], (g, right)).wait_recv()
            total = total + y_in[source].astype(f32)
        own_sum[...] = total

    for load in l_adam:
        load.wait()
    gradient = own_sum[...]

    updated, _, _ = optimizer_step(gradient, adam_in[0], adam_in[1], adam_in[2])

    mine = zh * CORE + core

    def row_copy(d, landed):
        to, source = lax.rem(zh + d, ZH), lax.rem(zh - d + ZH, ZH)
        block = fresh_rows.at[(source if landed else zh) * CORE + core]
        return remote(block, block, row_send.at[d], row_recv.at[d], (grp_of(y, to, core), t))

    fresh_rows[mine] = updated.astype(bf16)
    for d in FAR_Z:
        row_copy(d, False).start()
    store = pltpu.make_async_copy(own_sum, gradient_hbm, store_sem.at[0])
    store.start()
    decode_across(1 - core).wait_recv()
    decode = decode_all[...].reshape(CORE * Y * DECODE, WIDTH).astype(bf16)

    for name in order:
        piece(name, False).wait_send()
    totals_of_core.wait_send()
    for d in range(1, ZH):
        totals_over_z(d, False).wait_send()
    for d in range(1, Y):
        totals_over_y(d, False).wait_send()
        decode_copy(d, False).wait_send()
    decode_across(core).wait_send()
    for step in range(TP):
        if step == last:
            last_copy(0).wait_send()
            last_copy(1).wait_send()
        else:
            core_copy(step).wait_send()
        head = head_of(step)
        if step >= WIDE:
            for d in range(1, ZH):
                z_copy(step, d, False).wait_send()

        @pl.when(head != y)
        def _():
            (y_copy if step >= WIDE else wide_copy)(step, head).wait_send()

    @pl.when(early)
    def _():
        for d in range(1, ZH):
            z_copy(star, d, False).wait_send()

    for d in range(1, ZH):
        row_copy(d, True).wait_recv()

    part = dot(decode, fresh_rows[...].reshape(HEAD_SIZE, WIDTH), ((1,), (1,)))
    part_out[...] = part.reshape(CORE, Y, DECODE, HEAD_SIZE)

    def part_copy(of_core, d):
        to = lax.rem(y + d, Y)
        return remote(
            part_out.at[of_core, to],
            part_in.at[core, t],
            part_send.at[of_core * Y + to],
            part_recv.at[core * TP + t],
            (grp_of(to, zh, of_core), y),
        )

    for d in FAR_Y:
        part_copy(core, d).start()
        part_copy(1 - core, d).start()
    part_copy(1 - core, 0).start()

    @pl.when(t == y)
    def _():
        part_in[core, t] = part_out[core, y]

    @pl.when(t != y)
    def _():
        part_copy(core, 0).start()

    def part_arrived(of_core, d):
        source = lax.rem(t + d, TP)
        landed = part_in.at[of_core, source]
        remote(
            landed,
            landed,
            part_send.at[0],
            part_recv.at[of_core * TP + source],
            (grp_of(y, zh, 1 - core), t),
        ).wait_recv()

    for d in range(1, TP):
        part_arrived(core, d)
        part_arrived(1 - core, d)
    part_arrived(1 - core, 0)

    @pl.when(t != y)
    def _():
        part_arrived(core, 0)

    new_values = jnp.sum(part_in[...].reshape(CORE * TP, DECODE, HEAD_SIZE), axis=0)
    new_values = new_values.astype(bf16).astype(f32)
    outcome = cache_part[...] + own_part[...] * jnp.concatenate([new_values] * QUERIES, axis=0)
    attended[...] = jnp.concatenate(
        [outcome[j * DECODE : (j + 1) * DECODE] for j in range(QUERIES)], axis=1
    )
    result_store = pltpu.make_async_copy(attended, attended_hbm, store_sem.at[1])
    result_store.start()

    for d in range(1, ZH):
        row_copy(d, False).wait_send()
    for d in range(Y):
        part_copy(1 - core, d).wait_send()
    for d in range(1, Y):
        part_copy(core, d).wait_send()

    @pl.when(t != y)
    def _():
        part_copy(core, 0).wait_send()

    store.wait()
    result_store.wait()


def finish_kernel(gradient, master, one, two, attended, new_master, new_one, new_two, rounded):
    new_master[...], new_one[...], new_two[...] = optimizer_step(
        gradient[...], master[...], one[...], two[...]
    )
    rounded[...] = attended[...].astype(bf16)


def per_device(
    learn_rows,
    cot_values,
    rewards,
    group_ids,
    master,
    moment_one,
    moment_two,
    decode_rows,
    queries,
    fresh_keys,
    stored_keys,
    stored_values,
    cache_lengths,
):
    dma = pltpu.SemaphoreType.DMA
    shard = jax.ShapeDtypeStruct((BLOCK, WIDTH), f32)
    heads = QUERIES * HEAD_SIZE
    scratch = [
        ((ROWS, HEAD_SIZE), bf16),
        ((ROWS, WIDTH), bf16),
        ((ROWS // 128, 128), f32),
        ((ROWS // 128, 128), jnp.int32),
        ((3, BLOCK, WIDTH), f32),
        ((DECODE, WIDTH), bf16),
        ((DECODE, heads), bf16),
        ((DECODE, HEAD_SIZE), bf16),
        ((DECODE, SLOTS, HEAD_SIZE), bf16),
        ((DECODE, SLOTS, HEAD_SIZE), bf16),
        ((DECODE, heads), f32),
        ((TP * BLOCKS, BLOCK, ROWS), bf16),
        ((GROUPS, ROWS), bf16),
        ((3, 8, GROUPS), f32),
        ((8, GROUPS), f32),
        ((ZH, 8, GROUPS), f32),
        ((Y, 8, GROUPS), f32),
        ((CORE, Y, DECODE, WIDTH), f32),
        ((QUERIES * DECODE, SLOTS), bf16),
        ((QUERIES * DECODE, HEAD_SIZE), f32),
        ((QUERIES * DECODE, HEAD_SIZE), f32),
        ((TP, HALF, WIDTH), f32),
        ((TP, HALF, WIDTH), bf16),
        ((TP, HALF, WIDTH), bf16),
        ((TP, ZH, BLOCK, WIDTH), bf16),
        ((TP, ZH, BLOCK, WIDTH), bf16),
        ((TP, BLOCK, WIDTH), bf16),
        ((Y, BLOCK, WIDTH), bf16),
        ((WIDE, HALF, WIDTH), bf16),
        ((Y, HALF, WIDTH), bf16),
        ((BLOCK, WIDTH), f32),
        ((ZH * CORE, BLOCK, WIDTH), bf16),
        ((CORE, Y, DECODE, HEAD_SIZE), f32),
        ((CORE, TP, DECODE, HEAD_SIZE), f32),
    ]
    semaphores = [12, 2, 17, 17, TP + 1, TP + 1, TP * ZH, TP * ZH, TP, Y, ZH, ZH, CORE * Y, CORE * TP, ZH + Y, ZH + Y, Y, Y]
    hbm = pl.BlockSpec(memory_space=pltpu.HBM)
    gradient, attended = pl.pallas_call(
        kernel,
        out_shape=(shard, jax.ShapeDtypeStruct((DECODE, heads), f32)),
        in_specs=[hbm] * 12 + [pl.BlockSpec(memory_space=pltpu.SMEM)],
        out_specs=[hbm] * 2,
        scratch_shapes=[pltpu.VMEM(shape, kind) for shape, kind in scratch]
        + [dma((n,)) for n in semaphores],
        compiler_params=pltpu.CompilerParams(
            collective_id=0, has_side_effects=True, vmem_limit_bytes=60 * 1024 * 1024
        ),
    )(
        cot_values,
        learn_rows,
        rewards.reshape(ROWS // 128, 128),
        group_ids.reshape(ROWS // 128, 128),
        master,
        moment_one,
        moment_two,
        decode_rows,
        queries,
        fresh_keys,
        stored_keys,
        stored_values,
        cache_lengths,
    )
    return pl.pallas_call(
        finish_kernel,
        out_shape=(shard, shard, shard, jax.ShapeDtypeStruct((DECODE, heads), bf16)),
    )(gradient, master, moment_one, moment_two, attended)


def solution(mesh):
    shards, rows = P("grp", "tp"), P("grp")
    cache = P("grp", None, "tp")
    in_specs = (
        shards,
        shards,
        rows,
        rows,
        shards,
        shards,
        shards,
        P("grp", None),
        shards,
        shards,
        cache,
        cache,
        rows,
    )
    return jax.shard_map(
        per_device, mesh=mesh, in_specs=in_specs, out_specs=(shards,) * 4, check_vma=False
    )
```

```python
import math

import jax
import jax.numpy as jnp
from jax import lax
from jax.experimental import pallas as pl
from jax.experimental.pallas import tpu as pltpu
from jax.sharding import PartitionSpec as P

HEAD_SIZE = 128
QUERIES = 8
ROWS = 1536
WIDTH = 640
GROUPS = 256
SLOTS = 256
DECODE = 8
Y, ZH, CORE, X, ZL = 8, 4, 2, 4, 2
TP = X * ZL
BLOCKS = 8
BLOCK = 16
HALF = 64
WIDE = 4
FAR_Z = (2, 1, 3)
FAR_Y = (4, 3, 5, 2, 6, 1, 7)

beta_one = 0.9
beta_two = 0.95
learning_rate = 0.001
weight_decay = 0.1
adam_epsilon = 1e-08
step_count = 2.0

MESH = pl.DeviceIdType.MESH
bf16, f32 = jnp.bfloat16, jnp.float32


def split_three(value):
    high = value.astype(bf16)
    rest = value - high.astype(f32)
    middle = rest.astype(bf16)
    low = (rest - middle.astype(f32)).astype(bf16)
    return high, middle, low


def optimizer_step(gradient, master, moment_one, moment_two):
    first = beta_one * moment_one + (1.0 - beta_one) * gradient
    second = beta_two * moment_two + (1.0 - beta_two) * gradient * gradient
    first_hat = first / (1.0 - beta_one**step_count)
    second_hat = second / (1.0 - beta_two**step_count)
    updated = master - learning_rate * (
        first_hat / (jnp.sqrt(second_hat) + adam_epsilon) + weight_decay * master
    )
    return updated, first, second


def dot(a, b, dims):
    return lax.dot_general(a, b, (dims, ((), ())), preferred_element_type=f32)


def kernel(
    cot_hbm,
    learn_hbm,
    rewards_hbm,
    ids_hbm,
    master_hbm,
    one_hbm,
    two_hbm,
    decode_hbm,
    queries_hbm,
    fresh_hbm,
    keys_hbm,
    values_hbm,
    lengths_ref,
    gradient_hbm,
    attended_hbm,
    cot,
    learn,
    rewards,
    ids,
    adam_in,
    decode_own,
    queries,
    fresh,
    keys,
    values,
    attended,
    gathered,
    member,
    totals_out,
    totals_core,
    totals_z,
    totals_y,
    decode_all,
    weights,
    cache_part,
    own_part,
    kept,
    core_out,
    core_in,
    z_out,
    z_in,
    y_out,
    y_in,
    wide_out,
    wide_in,
    own_sum,
    fresh_rows,
    part_out,
    part_in,
    load_sem,
    store_sem,
    ag_send,
    ag_recv,
    core_send,
    core_recv,
    z_send,
    z_recv,
    y_send,
    y_recv,
    row_send,
    row_recv,
    part_send,
    part_recv,
    tot_send,
    tot_recv,
    dec_send,
    dec_recv,
):
    g, t = lax.axis_index("grp"), lax.axis_index("tp")
    y, zh, core = g // (ZH * CORE), lax.rem(g // CORE, ZH), lax.rem(g, CORE)
    x, zl = t // ZL, lax.rem(t, ZL)

    def grp_of(y_at, zh_at, core_at):
        return (y_at * ZH + zh_at) * CORE + core_at

    def tp_of(x_off, flip):
        return lax.rem(x + x_off + X, X) * ZL + lax.rem(zl + flip, ZL)

    right, left, across = tp_of(1, 0), tp_of(-1, 0), tp_of(0, 1)

    def remote(src, dst, send, recv, device):
        return pltpu.make_async_remote_copy(
            src_ref=src,
            dst_ref=dst,
            send_sem=send,
            recv_sem=recv,
            device_id=device,
            device_id_type=MESH,
        )

    loads = [
        (cot_hbm, cot),
        (ids_hbm, ids),
        (rewards_hbm, rewards),
        (queries_hbm, queries),
        (fresh_hbm, fresh),
        (keys_hbm, keys),
        (decode_hbm.at[:, pl.ds(pl.multiple_of(t * WIDTH, 128), WIDTH)], decode_own),
        (learn_hbm, learn),
        (values_hbm, values),
        (master_hbm, adam_in.at[0]),
        (one_hbm, adam_in.at[1]),
        (two_hbm, adam_in.at[2]),
    ]
    loads = [pltpu.make_async_copy(src, dst, load_sem.at[i]) for i, (src, dst) in enumerate(loads)]
    for load in loads[:3]:
        load.start()
    (l_cot, l_ids, l_rewards, l_queries, l_fresh, l_keys, l_decode, l_learn, l_values, *l_adam) = loads

    barrier = pltpu.get_barrier_semaphore()

    def greet(device):
        pl.semaphore_signal(barrier, inc=1, device_id=device, device_id_type=MESH)

    for peer in (right, left, across):
        greet((g, peer))
    greet((grp_of(y, zh, 1 - core), t))
    for d in range(1, ZH):
        greet((grp_of(y, lax.rem(zh + d, ZH), core), t))
    for d in range(1, Y):
        greet((grp_of(lax.rem(y + d, Y), zh, core), t))
    l_cot.wait()
    turned = cot[...].T
    gathered[pl.ds(t * BLOCKS, BLOCKS)] = turned.reshape(BLOCKS, BLOCK, ROWS)

    pl.semaphore_wait(barrier, 3 + 1 + (ZH - 1) + (Y - 1))

    xl, xr, xx = tp_of(-1, 0), tp_of(1, 0), tp_of(2, 0)
    zo, zxl, zxr, zxx = tp_of(0, 1), tp_of(-1, 1), tp_of(1, 1), tp_of(2, 1)
    pieces = {
        "z0": (across, t, zo, 4, 4),
        "z1": (across, t, zo, 0, 4),
        "z2": (across, xl, zxl, 0, 1),
        "z3": (across, xr, zxr, 0, 1),
        "z4": (across, xx, zxx, 0, 4),
        "r0": (right, t, xl, 0, 4),
        "r1": (right, t, xl, 4, 4),
        "r2": (right, xl, xx, 0, 4),
        "r3": (right, zo, zxl, 4, 4),
        "r4": (right, zo, zxl, 1, 3),
        "r5": (right, zxl, zxx, 4, 2),
        "l0": (left, t, xr, 4, 4),
        "l1": (left, t, xr, 0, 4),
        "l2": (left, xr, xx, 4, 4),
        "l3": (left, zo, zxr, 4, 4),
        "l4": (left, zo, zxr, 1, 3),
        "l5": (left, zxr, zxx, 6, 2),
    }
    order = list(pieces)

    def piece(name, landed):
        peer, source, lands, first, count = pieces[name]
        blocks = gathered.at[pl.ds((lands if landed else source) * BLOCKS + first, count)]
        n = order.index(name)
        return remote(blocks, blocks, ag_send.at[n], ag_recv.at[n], (g, peer))

    def send(*names):
        for name in names:
            piece(name, False).start()

    def arrived(*names):
        for name in names:
            piece(name, True).wait_recv()

    send("z0", "r0", "l0")
    for load in loads[3:]:
        load.start()

    l_ids.wait()
    l_rewards.wait()
    group_at = lax.broadcasted_iota(jnp.int32, (GROUPS, ROWS), 0)
    id_row = jnp.concatenate([ids[k : k + 1, :] for k in range(ROWS // 128)], axis=1)
    reward_row = jnp.concatenate([rewards[k : k + 1, :] for k in range(ROWS // 128)], axis=1)
    member[...] = jnp.where(group_at == id_row, 1.0, 0.0).astype(bf16)
    high, middle, low = split_three(reward_row)
    rows = lax.broadcasted_iota(jnp.int32, (8, ROWS), 0)
    stack = jnp.where(
        rows == 0,
        high.astype(f32),
        jnp.where(rows == 1, middle.astype(f32), jnp.where(rows == 2, low.astype(f32), 1.0)),
    )
    totals_out[0] = dot(stack.astype(bf16), member[...], ((1,), (1,)))
    totals_of_core = remote(
        totals_out.at[0], totals_core, tot_send.at[0], tot_recv.at[0], (grp_of(y, zh, 1 - core), t)
    )
    totals_of_core.start()
    send("r1", "l1")

    totals_of_core.wait_recv()
    totals_out[1] = totals_out[0] + totals_core[...]

    def totals_over_z(d, landed):
        to, source = lax.rem(zh + d, ZH), lax.rem(zh - d + ZH, ZH)
        return remote(
            totals_out.at[1],
            totals_z.at[source if landed else zh],
            tot_send.at[d],
            tot_recv.at[d],
            (grp_of(y, to, core), t),
        )

    for d in FAR_Z:
        totals_over_z(d, False).start()
    send("z1")

    total = totals_out[1]
    for d in range(1, ZH):
        totals_over_z(d, True).wait_recv()
        total = total + totals_z[lax.rem(zh - d + ZH, ZH)]
    totals_out[2] = total

    def totals_over_y(d, landed):
        to, source = lax.rem(y + d, Y), lax.rem(y - d + Y, Y)
        return remote(
            totals_out.at[2],
            totals_y.at[source if landed else y],
            tot_send.at[ZH + d],
            tot_recv.at[ZH + d],
            (grp_of(to, zh, core), t),
        )

    for d in FAR_Y:
        totals_over_y(d, False).start()

    l_decode.wait()
    decode_all[core, y] = decode_own[...].astype(f32)

    def decode_copy(d, landed):
        to, source = lax.rem(y + d, Y), lax.rem(y - d + Y, Y)
        block = decode_all.at[core, source if landed else y]
        return remote(block, block, dec_send.at[d], dec_recv.at[d], (grp_of(to, zh, core), t))

    for d in range(1, Y):
        decode_copy(d, False).start()

    arrived("r0")
    send("r2", "z2")
    arrived("l0")
    send("l2")

    l_queries.wait()
    l_fresh.wait()
    l_keys.wait()
    scale = 1.0 / math.sqrt(HEAD_SIZE)
    tiles = queries[...].astype(f32)
    tiles = jnp.concatenate(
        [tiles[:, j * HEAD_SIZE : (j + 1) * HEAD_SIZE] for j in range(QUERIES)], axis=0
    )
    query_rows = tiles.astype(bf16)
    row_of = lax.broadcasted_iota(jnp.int32, (QUERIES * DECODE, SLOTS), 0) & (DECODE - 1)
    slot_of = lax.broadcasted_iota(jnp.int32, (QUERIES * DECODE, SLOTS), 1)
    scores = jnp.zeros((QUERIES * DECODE, SLOTS), f32)
    for r in range(DECODE):
        of_row = dot(query_rows, keys[r], ((1,), (1,))) * scale
        of_row = jnp.where(slot_of < lengths_ref[r], of_row, -jnp.inf)
        scores = jnp.where(row_of == r, of_row, scores)
    fresh_tiles = jnp.concatenate([fresh[...].astype(f32)] * QUERIES, axis=0)
    own_score = jnp.sum(tiles * fresh_tiles, axis=1, keepdims=True) * scale
    highest = jnp.maximum(jnp.max(scores, axis=1, keepdims=True), own_score)
    cache_exp = jnp.exp(scores - highest)
    own_exp = jnp.exp(own_score - highest)
    denominator = jnp.sum(cache_exp, axis=1, keepdims=True) + own_exp
    weights[...] = (cache_exp / denominator).astype(bf16)
    own_weight = (own_exp / denominator).astype(bf16).astype(f32)
    own_part[...] = jnp.broadcast_to(own_weight, (QUERIES * DECODE, HEAD_SIZE))

    l_values.wait()
    row_at = lax.broadcasted_iota(jnp.int32, (QUERIES * DECODE, HEAD_SIZE), 0) & (DECODE - 1)
    cached = jnp.zeros((QUERIES * DECODE, HEAD_SIZE), f32)
    for r in range(DECODE):
        of_row = dot(weights[...], values[r], ((1,), (0,)))
        cached = jnp.where(row_at == r, of_row, cached)
    cache_part[...] = cached

    for owner in range(ZH):
        fresh_rows[owner * CORE + 1 - core] = jnp.zeros((BLOCK, WIDTH), bf16)

    for d in range(1, Y):
        totals_over_y(d, True).wait_recv()
        total = total + totals_y[lax.rem(y - d + Y, Y)]

    size = total[3:4]
    mean = jnp.where(
        size > 0.5, (total[0:1] + total[1:2] + total[2:3]) / jnp.maximum(size, 1.0), 0.0
    )
    high, middle, low = split_three(mean)
    rows = lax.broadcasted_iota(jnp.int32, (8, GROUPS), 0)
    stack = jnp.where(
        rows == 0,
        high.astype(f32),
        jnp.where(rows == 1, middle.astype(f32), jnp.where(rows == 2, low.astype(f32), 0.0)),
    )
    means = dot(stack.astype(bf16), member[...], ((1,), (0,)))
    advantage = (reward_row - (means[0:1] + means[1:2] + means[2:3])) / float(ROWS)
    l_learn.wait()
    for k in range(ROWS // 128):
        column = jnp.broadcast_to(advantage[:, k * 128 : (k + 1) * 128], (128, 128)).T
        scaled = learn[k * 128 : (k + 1) * 128, :].astype(f32) * jnp.concatenate(
            [column] * (WIDTH // 128), axis=1
        )
        learn[k * 128 : (k + 1) * 128, :] = scaled.astype(bf16)

    def head_of(step):
        x_off = jnp.where(
            jnp.logical_or(step == 1, step == 5),
            X - 1,
            jnp.where(
                jnp.logical_or(step == 2, step == 6),
                1,
                jnp.where(jnp.logical_or(step == 4, step == 7), 2, 0),
            ),
        )
        flip = jnp.where(jnp.logical_or(step == 3, step >= 5), 1, 0)
        return tp_of(x_off, flip)

    def core_copy(step):
        return remote(
            core_out.at[step],
            core_in.at[step],
            core_send.at[step],
            core_recv.at[step],
            (grp_of(y, zh, 1 - core), t),
        )

    def z_copy(step, d, landed):
        to, source = lax.rem(zh + d, ZH), lax.rem(zh - d + ZH, ZH)
        return remote(
            z_out.at[step, to],
            z_in.at[step, source if landed else zh],
            z_send.at[step * ZH + d],
            z_recv.at[step * ZH + d],
            (grp_of(y, to, core), t),
        )

    def y_copy(step, head):
        return remote(
            y_out.at[step], y_in.at[y], y_send.at[step], y_recv.at[y], (grp_of(head, zh, core), t)
        )

    def wide_copy(step, head):
        return remote(
            wide_out.at[step], wide_in.at[y], y_send.at[step], y_recv.at[y], (grp_of(head, zh, core), t)
        )

    star = jnp.where(
        y == head_of(0), 0, jnp.where(y == head_of(1), 1, jnp.where(y == head_of(2), 2, 3))
    )
    early = jnp.logical_or(star < 3, y == head_of(3))

    def over_z(step, block):
        kept[step] = block
        z_out[step] = block.astype(bf16).reshape(ZH, BLOCK, WIDTH)
        for d in FAR_Z:
            z_copy(step, d, False).start()

    def z_total(step):
        total = kept[step, pl.ds(pl.multiple_of(zh * BLOCK, BLOCK), BLOCK)]
        for d in range(1, ZH):
            z_copy(step, d, True).wait_recv()
            total = total + z_in[step, lax.rem(zh - d + ZH, ZH)].astype(f32)
        return total

    def from_core(step):
        core_copy(step).wait_recv()
        over_z(step, kept[step] + core_in[step].astype(f32))

    def from_core_wide(step):
        core_copy(step).wait_recv()
        both = kept[step] + core_in[step].astype(f32)
        kept[step] = both
        head = head_of(step)

        @pl.when(head != y)
        def _():
            wide_out[step] = both.astype(bf16)
            wide_copy(step, head).start()

    def from_z(step, _):
        total = z_total(step)
        head = head_of(step)

        @pl.when(head == y)
        def _():
            own_sum[...] = total

        @pl.when(head != y)
        def _():
            y_out[step] = total.astype(bf16)
            y_copy(step, head).start()

        return 0

    def rows_of(step, parity):
        base = head_of(step) * BLOCKS
        return [gathered[base + 2 * k + parity] for k in range(ZH)]

    last = TP - 1
    quarter = HALF // 2

    def last_copy(half):
        rows = pl.ds(half * quarter, quarter)
        return remote(
            core_out.at[last, rows],
            core_in.at[last, rows],
            core_send.at[last + half],
            core_recv.at[last + half],
            (grp_of(y, zh, 1 - core), t),
        )

    def multiply_last(half):
        chosen = slice(half * (ZH // 2), (half + 1) * (ZH // 2))
        lhs = rows_of(last, 1 - core)[chosen] + rows_of(last, core)[chosen]
        result = dot(jnp.concatenate(lhs, axis=0), learn[...], ((1,), (0,)))
        rows = slice(half * quarter, (half + 1) * quarter)
        core_out[last, rows] = result[:quarter].astype(bf16)
        last_copy(half).start()
        kept[last, rows] = result[quarter:]

    def from_core_last(half):
        last_copy(half).wait_recv()
        rows = slice(half * quarter, (half + 1) * quarter)
        both = kept[last, rows] + core_in[last, rows].astype(f32)
        kept[last, rows] = both
        blocks = slice(half * (ZH // 2), (half + 1) * (ZH // 2))
        z_out[last, blocks] = both.astype(bf16).reshape(ZH // 2, BLOCK, WIDTH)
        for d in FAR_Z:
            to = lax.rem(zh + d, ZH)

            @pl.when((to >= ZH // 2) if half else (to < ZH // 2))
            def _():
                z_copy(last, d, False).start()

    def multiply(heads):
        lhs = [rows_of(head, 1 - core) + rows_of(head, core) for head in heads]
        result = dot(jnp.concatenate(sum(lhs, []), axis=0), learn[...], ((1,), (0,)))
        for n, head in enumerate(heads):
            core_out[head] = result[2 * n * HALF : (2 * n + 1) * HALF].astype(bf16)
            core_copy(head).start()
            kept[head] = result[(2 * n + 1) * HALF : (2 * n + 2) * HALF]

    def decode_across(at):
        block = decode_all.at[at]
        return remote(block, block, dec_send.at[0], dec_recv.at[0], (grp_of(y, zh, 1 - core), t))

    def one_step(step, _):
        @pl.when(step == 0)
        def _():
            arrived("r1")

        @pl.when(step == 1)
        def _():
            arrived("z0")
            send("r3", "l3")
            arrived("l1")
            send("z3")
            arrived("z1")
            send("r4", "l4")

        @pl.when(step == 2)
        def _():
            arrived("r2", "l2")
            send("z4")

        @pl.when(step == 3)
        def _():
            arrived("r3", "l3")
            send("r5", "l5")
            for d in range(1, Y):
                decode_copy(d, True).wait_recv()
            decode_across(core).start()
            arrived("r4", "z2", "l4", "z3")

        first = 2 * step - jnp.where(step >= 3, 1, 0)

        @pl.when(step == 2)
        def _():
            multiply([first])

        @pl.when(step != 2)
        def _():
            multiply([first, first + 1])

        @pl.when(step == 1)
        def _():
            from_core_wide(0)
            from_core_wide(1)

        @pl.when(step == 2)
        def _():
            from_core_wide(2)
            from_core_wide(3)

        @pl.when(step == 3)
        def _():
            from_core(4)

        return 0

    lax.fori_loop(0, 4, one_step, 0)
    arrived("z4")
    multiply_last(0)
    from_core(5)
    from_core(6)
    from_z(4, 0)
    from_core_last(0)
    arrived("r5", "l5")
    multiply_last(1)

    from_core_last(1)

    lax.fori_loop(5, TP - 1, from_z, 0)

    @pl.when(early)
    def _():
        block = kept[star]
        for d in range(1, Y):
            source = lax.rem(y - d + Y, Y)
            landed = wide_in.at[source]
            remote(landed, landed, y_send.at[0], y_recv.at[source], (g, right)).wait_recv()
            block = block + wide_in[source].astype(f32)
        over_z(star, block)

    from_z(TP - 1, 0)

    @pl.when(early)
    def _():
        own_sum[...] = z_total(star)

    @pl.when(jnp.logical_not(early))
    def _():
        total = own_sum[...]
        for d in range(1, Y):
            source = lax.rem(y - d + Y, Y)
            landed = y_in.at[source]
            remote(landed, landed, y_send.at[0], y_recv.at[source], (g, right)).wait_recv()
            total = total + y_in[source].astype(f32)
        own_sum[...] = total

    for load in l_adam:
        load.wait()
    gradient = own_sum[...]

    updated, _, _ = optimizer_step(gradient, adam_in[0], adam_in[1], adam_in[2])

    mine = zh * CORE + core

    def row_copy(d, landed):
        to, source = lax.rem(zh + d, ZH), lax.rem(zh - d + ZH, ZH)
        block = fresh_rows.at[(source if landed else zh) * CORE + core]
        return remote(block, block, row_send.at[d], row_recv.at[d], (grp_of(y, to, core), t))

    fresh_rows[mine] = updated.astype(bf16)
    for d in FAR_Z:
        row_copy(d, False).start()
    store = pltpu.make_async_copy(own_sum, gradient_hbm, store_sem.at[0])
    store.start()
    decode_across(1 - core).wait_recv()
    decode = decode_all[...].reshape(CORE * Y * DECODE, WIDTH).astype(bf16)

    for name in order:
        piece(name, False).wait_send()
    totals_of_core.wait_send()
    for d in range(1, ZH):
        totals_over_z(d, False).wait_send()
    for d in range(1, Y):
        totals_over_y(d, False).wait_send()
        decode_copy(d, False).wait_send()
    decode_across(core).wait_send()
    for step in range(TP):
        if step == last:
            last_copy(0).wait_send()
            last_copy(1).wait_send()
        else:
            core_copy(step).wait_send()
        head = head_of(step)
        if step >= WIDE:
            for d in range(1, ZH):
                z_copy(step, d, False).wait_send()

        @pl.when(head != y)
        def _():
            (y_copy if step >= WIDE else wide_copy)(step, head).wait_send()

    @pl.when(early)
    def _():
        for d in range(1, ZH):
            z_copy(star, d, False).wait_send()

    for d in range(1, ZH):
        row_copy(d, True).wait_recv()

    part = dot(decode, fresh_rows[...].reshape(HEAD_SIZE, WIDTH), ((1,), (1,)))
    part_out[...] = part.reshape(CORE, Y, DECODE, HEAD_SIZE)

    def part_copy(of_core, d):
        to = lax.rem(y + d, Y)
        return remote(
            part_out.at[of_core, to],
            part_in.at[core, t],
            part_send.at[of_core * Y + to],
            part_recv.at[core * TP + t],
            (grp_of(to, zh, of_core), y),
        )

    for d in FAR_Y:
        part_copy(core, d).start()
        part_copy(1 - core, d).start()
    part_copy(1 - core, 0).start()

    @pl.when(t == y)
    def _():
        part_in[core, t] = part_out[core, y]

    @pl.when(t != y)
    def _():
        part_copy(core, 0).start()

    def part_arrived(of_core, d):
        source = lax.rem(t + d, TP)
        landed = part_in.at[of_core, source]
        remote(
            landed,
            landed,
            part_send.at[0],
            part_recv.at[of_core * TP + source],
            (grp_of(y, zh, 1 - core), t),
        ).wait_recv()

    for d in range(1, TP):
        part_arrived(core, d)
        part_arrived(1 - core, d)
    part_arrived(1 - core, 0)

    @pl.when(t != y)
    def _():
        part_arrived(core, 0)

    new_values = jnp.sum(part_in[...].reshape(CORE * TP, DECODE, HEAD_SIZE), axis=0)
    new_values = new_values.astype(bf16).astype(f32)
    outcome = cache_part[...] + own_part[...] * jnp.concatenate([new_values] * QUERIES, axis=0)
    attended[...] = jnp.concatenate(
        [outcome[j * DECODE : (j + 1) * DECODE] for j in range(QUERIES)], axis=1
    )
    result_store = pltpu.make_async_copy(attended, attended_hbm, store_sem.at[1])
    result_store.start()

    for d in range(1, ZH):
        row_copy(d, False).wait_send()
    for d in range(Y):
        part_copy(1 - core, d).wait_send()
    for d in range(1, Y):
        part_copy(core, d).wait_send()

    @pl.when(t != y)
    def _():
        part_copy(core, 0).wait_send()

    store.wait()
    result_store.wait()


def finish_kernel(gradient, master, one, two, attended, new_master, new_one, new_two, rounded):
    new_master[...], new_one[...], new_two[...] = optimizer_step(
        gradient[...], master[...], one[...], two[...]
    )
    rounded[...] = attended[...].astype(bf16)


def per_device(
    learn_rows,
    cot_values,
    rewards,
    group_ids,
    master,
    moment_one,
    moment_two,
    decode_rows,
    queries,
    fresh_keys,
    stored_keys,
    stored_values,
    cache_lengths,
):
    dma = pltpu.SemaphoreType.DMA
    shard = jax.ShapeDtypeStruct((BLOCK, WIDTH), f32)
    heads = QUERIES * HEAD_SIZE
    scratch = [
        ((ROWS, HEAD_SIZE), bf16),
        ((ROWS, WIDTH), bf16),
        ((ROWS // 128, 128), f32),
        ((ROWS // 128, 128), jnp.int32),
        ((3, BLOCK, WIDTH), f32),
        ((DECODE, WIDTH), bf16),
        ((DECODE, heads), bf16),
        ((DECODE, HEAD_SIZE), bf16),
        ((DECODE, SLOTS, HEAD_SIZE), bf16),
        ((DECODE, SLOTS, HEAD_SIZE), bf16),
        ((DECODE, heads), f32),
        ((TP * BLOCKS, BLOCK, ROWS), bf16),
        ((GROUPS, ROWS), bf16),
        ((3, 8, GROUPS), f32),
        ((8, GROUPS), f32),
        ((ZH, 8, GROUPS), f32),
        ((Y, 8, GROUPS), f32),
        ((CORE, Y, DECODE, WIDTH), f32),
        ((QUERIES * DECODE, SLOTS), bf16),
        ((QUERIES * DECODE, HEAD_SIZE), f32),
        ((QUERIES * DECODE, HEAD_SIZE), f32),
        ((TP, HALF, WIDTH), f32),
        ((TP, HALF, WIDTH), bf16),
        ((TP, HALF, WIDTH), bf16),
        ((TP, ZH, BLOCK, WIDTH), bf16),
        ((TP, ZH, BLOCK, WIDTH), bf16),
        ((TP, BLOCK, WIDTH), bf16),
        ((Y, BLOCK, WIDTH), bf16),
        ((WIDE, HALF, WIDTH), bf16),
        ((Y, HALF, WIDTH), bf16),
        ((BLOCK, WIDTH), f32),
        ((ZH * CORE, BLOCK, WIDTH), bf16),
        ((CORE, Y, DECODE, HEAD_SIZE), f32),
        ((CORE, TP, DECODE, HEAD_SIZE), f32),
    ]
    semaphores = [12, 2, 17, 17, TP + 1, TP + 1, TP * ZH, TP * ZH, TP, Y, ZH, ZH, CORE * Y, CORE * TP, ZH + Y, ZH + Y, Y, Y]
    hbm = pl.BlockSpec(memory_space=pltpu.HBM)
    gradient, attended = pl.pallas_call(
        kernel,
        out_shape=(shard, jax.ShapeDtypeStruct((DECODE, heads), f32)),
        in_specs=[hbm] * 12 + [pl.BlockSpec(memory_space=pltpu.SMEM)],
        out_specs=[hbm] * 2,
        scratch_shapes=[pltpu.VMEM(shape, kind) for shape, kind in scratch]
        + [dma((n,)) for n in semaphores],
        compiler_params=pltpu.CompilerParams(
            collective_id=0, has_side_effects=True, vmem_limit_bytes=60 * 1024 * 1024
        ),
    )(
        cot_values,
        learn_rows,
        rewards.reshape(ROWS // 128, 128),
        group_ids.reshape(ROWS // 128, 128),
        master,
        moment_one,
        moment_two,
        decode_rows,
        queries,
        fresh_keys,
        stored_keys,
        stored_values,
        cache_lengths,
    )
    return pl.pallas_call(
        finish_kernel,
        out_shape=(shard, shard, shard, jax.ShapeDtypeStruct((DECODE, heads), bf16)),
    )(gradient, master, moment_one, moment_two, attended)


def solution(mesh):
    shards, rows = P("grp", "tp"), P("grp")
    cache = P("grp", None, "tp")
    in_specs = (
        shards,
        shards,
        rows,
        rows,
        shards,
        shards,
        shards,
        P("grp", None),
        shards,
        shards,
        cache,
        cache,
        rows,
    )
    return jax.shard_map(
        per_device, mesh=mesh, in_specs=in_specs, out_specs=(shards,) * 4, check_vma=False
    )
```
